512 devices in a mesh: sfc: 128 (over y, z, core), blk: 4 (over x).
Axes of the slice: x: 4, y: 4, z: 16, core: 2. Of those that a mesh axis runs over, the one named last changes fastest.
Arguments:
- adjoint: float32 [5, 2048, 64, 128], P(None, 'sfc', 'blk'), may hold values from -6 to 6
- source: float32 [5, 2048, 64, 128], P(None, 'sfc', 'blk'), may hold values from -12 to 12
- velocity: bfloat16 [3, 2048, 64, 128], P(None, 'sfc', 'blk'), may hold values from -5 to 5
- dissip: bfloat16 [2048, 64, 128], P('sfc', 'blk'), may hold values from 0.5 to 2
- jacobian: float32 [3, 5, 5], replicated, may hold values from -2.5 to 2.5
- cut_counts: int32 [4096], P(('sfc', 'blk')), may hold values from 0 to 64, as said below
- cut_cell: int32 [262144], P(('sfc', 'blk')), may hold values from 0 to 4095
- face_angles: float32 [2, 262144], P(None, ('sfc', 'blk')), may hold values from -3.140625 to 3.140625
- face_area: float32 [262144], P(('sfc', 'blk')), may hold values from 0.2 to 1
- face_pressure: float32 [262144], P(('sfc', 'blk')), may hold values from 0.5 to 2
- tri_owner: int32 [262144, 1], P(('sfc', 'blk')), may hold values from 0 to 511; in each aligned block of 512 rows (0 to 511, 512 to 1023, ...) at most 2 rows name the same one
- tri_local: int32 [262144], P(('sfc', 'blk')), may hold values from 0 to 255
Outputs:
- relaxed: float32 [5, 2048, 64, 128], P(None, 'sfc', 'blk')
- sensitivity: float32 [3, 131072], P(None, ('sfc', 'blk'))
The draws below stay inside these ranges and needn't reach their ends.
Inputs may be any that keep to these rules, and one draw needn't show every extreme that they name: `cut_counts`: each brick has at most 64 live cut faces; some brick has exactly 64, some have none. `tri_owner`: among the cut-face slots of one device (aligned blocks of 512 rows) no owner is named more than 2 times.
All inputs are finite; a program needn't handle non-finite values.
Results may differ from the reference program's by a relative error of at most 0.00065.
Values sent between devices are 32-bit elements; how exact they have to be, the bound alone decides.
No kernel may reach another device: no remote copies, remote signals or barrier semaphores. Data moves between devices by JAX's collectives and lax.ppermute only.
A program may use at most 192 MiB of HBM per device.

```python
import math
import jax
import jax.numpy as jnp
import numpy as np
from jax import lax

BZ = 8
FPB = 64
TRI_DEV = 256
ITERS = 2
NX = 2048
NY = 64
NZ = 128
BRICKS = 4096
FACES = 262144
TRIS = 131072
CAP = 2
N_BLK = 4
DEVICES = 512


def draw_cut_counts(key, part):
    key = jax.random.fold_in(key, 11)
    second = jax.random.fold_in(key, 1)
    third = jax.random.fold_in(key, 2)
    fourth = jax.random.fold_in(key, 3)
    brick_cut = jax.random.randint(second, (BRICKS,), 0, 8)
    counts = jax.random.randint(third, (BRICKS,), FPB // 2, FPB + 1)
    counts = jnp.where(brick_cut > 0, counts, 0)
    pick = jax.random.randint(fourth, (), 0, BRICKS)
    counts = counts.at[pick].set(FPB)
    counts = counts.at[(pick + 1) % BRICKS].set(0)
    return counts.astype(jnp.int32)


def set_ends(drawn, key, least, largest):
    extent = drawn.shape
    place = [jax.random.randint(jax.random.fold_in(key, axis), (), 0, extent[axis]) for axis in range(len(extent))]
    drawn = drawn.at[tuple(place)].set(least)
    longest = extent.index(max(extent))
    place[longest] = (place[longest] + 1) % extent[longest]
    return drawn.at[tuple(place)].set(largest)


def levels(stream_key, dims, cuts, smallest, largest):
    def one(dim, blocks):
        heights = jax.random.uniform(jax.random.fold_in(jax.random.fold_in(stream_key, 6), dim), (blocks,), jnp.float32, smallest / len(cuts), largest / len(cuts))
        return jnp.repeat(jnp.exp(heights), dims[dim] // blocks).reshape((-1,) + (1,) * (len(dims) - dim - 1))

    factor_of = one(*cuts[0])
    for cut in cuts[1:]:
        factor_of = factor_of * one(*cut)
    return factor_of


def shared_out(stream_key, own, number, rows, number_of, top, reach, skew):
    order = jax.random.permutation(stream_key, number_of)
    heavy_load, usual = portions_of(number_of, rows * top, reach, skew, True), portions_of(number_of, rows * top, reach, skew, False)
    places = jnp.arange(number_of)

    def named(sizes, turn):
        used = int((sizes > 0).sum())
        fixed = max(1, used // 4)
        shifted = fixed + (places - fixed + turn * (used - fixed)) % max(1, number_of - fixed)
        return jnp.zeros((number_of,), jnp.int32).at[order[jnp.where(places < fixed, places, shifted)]].set(jnp.asarray(sizes, jnp.int32))

    sizes = jnp.where(number % 4 == 0, named(heavy_load, number // 4), named(usual, number - number // 4 - 1))
    mixed = jax.random.permutation(jax.random.fold_in(own, 3), number_of)
    source_of, taker = mixed[0:number_of // 2 * 2:2], mixed[1:number_of // 2 * 2:2]
    margin = jnp.minimum(sizes[source_of] - 1, reach - sizes[taker]) // 2
    margin = jnp.where((source_of == order[0]) | (taker == order[0]) | (sizes[taker] == 0), 0, jnp.maximum(margin, 0))
    shifted = jax.random.randint(jax.random.fold_in(own, 4), (number_of // 2,), 0, 1 << 20) % (margin + 1)
    sizes = sizes.at[source_of].add(-shifted).at[taker].add(shifted)
    members = jnp.searchsorted(jnp.cumsum(sizes), jnp.arange(rows * top), side="right").astype(jnp.int32)
    grid = members.reshape(top, rows).T
    grid = grid[jax.random.permutation(jax.random.fold_in(own, 1), rows)]
    turn = jax.random.randint(jax.random.fold_in(own, 2), (rows, 1), 0, top)
    return jnp.take_along_axis(grid, (jnp.arange(top)[None, :] + turn) % top, axis=1)


def portions_of(amount, total, most, lean, full):
    weights = [(1 << 20) // math.isqrt(standing ** lean) + 1 for standing in range(1, amount + 1)]
    largest = most if full else min(most, max(-(-total // amount), total * weights[0] // sum(weights)))
    least = 1 if total - largest >= amount - 1 else 0
    given, spare = [largest] + [least] * (amount - 1), total - largest - least * (amount - 1)
    while spare > 0:
        candidates = [i for i in range(1, amount) if given[i] < largest] or [i for i in range(1, amount) if given[i] < most]
        whole, budget = sum([weights[i] for i in candidates]), spare
        for i in candidates:
            more = min(most - given[i], max(1, budget * weights[i] // whole), spare)
            given[i] = given[i] + more
            spare = spare - more
    return np.array(given)


def scatter_about(own_key, shape, deviation, bound, shards=(), held_as=jnp.bfloat16):
    drawn = jax.random.normal(own_key, shape, jnp.float32) * deviation
    if len(shards) > 0:
        drawn = levels(own_key, shape, shards, -0.22, 0.18) * drawn
    return jnp.clip(drawn, min=-bound, max=bound).astype(held_as)


def setup_inputs(seed: int = 0) -> dict:
    key_of = jax.random.split(jax.random.key(seed), 13)
    adjoint = scatter_about(key_of[0], (5, NX, NY, NZ), 1.0, 6.0, ((1, 128), (2, 4)), jnp.float32)
    source = scatter_about(key_of[1], (5, NX, NY, NZ), 2.0, 12.0, ((1, 128), (2, 4)), jnp.float32)
    velocity = scatter_about(key_of[2], (3, NX, NY, NZ), 1.0, 5.0, ((1, 128), (2, 4)))
    dissip = jnp.clip(jnp.exp(math.log(2.0) - 1.3862944 * jax.random.uniform(key_of[3], (NX, NY, NZ), jnp.float32) ** levels(key_of[3], (NX, NY, NZ), ((0, 128), (1, 4)), -0.2, 0.2)), 0.5, 2.0).astype(jnp.bfloat16)
    jacobian = scatter_about(key_of[4], (3, 5, 5), 5 ** -0.5, 2.5, (), jnp.float32)
    cut_counts = draw_cut_counts(jax.random.fold_in(key_of[12], 71), 0)
    cut_cell = set_ends(jax.random.randint(key_of[6], (FACES,), 0, 4096), jax.random.fold_in(key_of[6], 1), 0, 4095).astype(jnp.int32)
    face_angles = jnp.clip(jax.random.uniform(key_of[7], (2, FACES), jnp.float32, -3.140625, 3.140625), -3.140625, 3.140625)
    face_area = jnp.clip(jnp.exp(math.log(1.0) - 1.609438 * jax.random.uniform(key_of[8], (FACES,), jnp.float32) ** levels(key_of[8], (FACES,), ((0, 512),), -0.2, 0.2)), 0.2, 1.0)
    face_pressure = jnp.clip(0.5 + 1.5 * jax.random.uniform(key_of[9], (FACES,), jnp.float32) ** levels(key_of[9], (FACES,), ((0, 512),), -0.2, 0.2), 0.5, 2.0)
    tri_owner_keys = jax.random.split(jax.random.fold_in(key_of[10], 1), FACES // (BZ * FPB))
    tri_owner_turns = jax.random.permutation(jax.random.fold_in(key_of[10], 3), FACES // (BZ * FPB))
    tri_owner = jax.vmap(lambda own, number: shared_out(jax.random.fold_in(key_of[10], 2), own, number, BZ * FPB, DEVICES, 1, CAP, 2))(tri_owner_keys, tri_owner_turns).reshape((FACES, 1))
    tri_local = set_ends(jax.random.randint(key_of[11], (FACES,), 0, TRI_DEV), jax.random.fold_in(key_of[11], 1), 0, TRI_DEV - 1).astype(jnp.int32)
    return {"adjoint": adjoint, "source": source, "velocity": velocity, "dissip": dissip, "jacobian": jacobian, "cut_counts": cut_counts, "cut_cell": cut_cell, "face_angles": face_angles, "face_area": face_area, "face_pressure": face_pressure, "tri_owner": tri_owner, "tri_local": tri_local}


OMEGA = 0.8


def face_normals(face_angles):
    first = face_angles[0]
    second = face_angles[1]
    return jnp.stack([jnp.cos(first) * jnp.cos(second), jnp.sin(first) * jnp.cos(second), jnp.sin(second)])


def apply_stencil(padded, field, velocity, dissip, jacobian):
    speeds = velocity.astype(jnp.float32)
    damping = dissip.astype(jnp.float32)
    pairs = ((padded[:, 2:, 1:-1, 1:-1], padded[:, :-2, 1:-1, 1:-1]),
             (padded[:, 1:-1, 2:, 1:-1], padded[:, 1:-1, :-2, 1:-1]),
             (padded[:, 1:-1, 1:-1, 2:], padded[:, 1:-1, 1:-1, :-2]))
    centre = jnp.zeros_like(field)
    beside = jnp.zeros_like(field)
    for direction in range(3):
        upper, lower = pairs[direction]
        turned = jnp.einsum('kc,kxyz->cxyz', jacobian[direction], upper - lower, precision=lax.Precision.HIGHEST)
        centre = centre + 0.5 * speeds[direction] * turned
        beside = beside + upper + lower
    return centre + damping * (6.0 * field - beside)


def wall_term(field, cells, normal, weight):
    flat = field[1:4].reshape(3, -1)
    momentum = flat[:, cells]
    project = jnp.sum(normal * momentum, axis=0)
    push = normal * (weight * project)
    total = jnp.zeros(flat.shape, jnp.float32).at[:, cells].add(push)
    blank = jnp.zeros((1, flat.shape[1]), jnp.float32)
    return jnp.concatenate([blank, total, blank], axis=0).reshape(field.shape)


def sweep(field, padded, source, velocity, dissip, jacobian, cells, normal, weight):
    applied = apply_stencil(padded, field, velocity, dissip, jacobian) + wall_term(field, cells, normal, weight)
    diagonal = 6.0 * dissip.astype(jnp.float32) + 1.0
    return field + OMEGA * (source - applied) / diagonal


def reference(adjoint, source, velocity, dissip, jacobian, cut_counts, cut_cell, face_angles, face_area, face_pressure, tri_owner, tri_local):
    position = jnp.arange(FACES, dtype=jnp.int32)
    live = (position % FPB < jnp.repeat(cut_counts, FPB)).astype(jnp.float32)
    device = position // (BZ * FPB)
    brick = (position // FPB) % BZ
    row_sfc = device // N_BLK
    row_blk = device % N_BLK
    gx = row_sfc * 16 + cut_cell // 256
    gy = row_blk * 16 + (cut_cell // 16) % 16
    gz = brick * 16 + cut_cell % 16
    cells = ((gx * NY + gy) * NZ + gz).astype(jnp.int32)
    normal = face_normals(face_angles)
    weight = face_area * live
    field = adjoint
    for step in range(ITERS):
        padded = jnp.pad(field, ((0, 0), (1, 1), (1, 1), (1, 1)))
        field = sweep(field, padded, source, velocity, dissip, jacobian, cells, normal, weight)
    momentum = field[1:4].reshape(3, -1)[:, cells]
    project = jnp.sum(normal * momentum, axis=0)
    term = normal * (face_pressure * weight * project)
    target = (tri_owner[:, 0] * TRI_DEV + tri_local).astype(jnp.int32)
    sensitivity = jnp.zeros((3, TRIS), jnp.float32).at[:, target].add(term)
    return field, sensitivity
```

```python
import functools

import jax
import jax.numpy as jnp
from jax import lax
from jax.experimental import pallas as pl
from jax.experimental.pallas import tpu as pltpu
from jax.sharding import PartitionSpec as P

TRI_DEV = 256
OMEGA = 0.8
BIG = pltpu.CompilerParams(vmem_limit_bytes=40 * 1024 * 1024)


def dot_last(a, b):
    return lax.dot_general(a, b, (((1,), (1,)), ((), ())), preferred_element_type=jnp.float32)


def halves(x):
    high = x.astype(jnp.bfloat16)
    return high, (x - high.astype(jnp.float32)).astype(jnp.bfloat16)


def relax_factor(damping):
    return OMEGA / (6.0 * damping + 1.0)


def face_normals(angles):
    cosine = jnp.cos(angles)
    sine = jnp.sin(angles)
    across = cosine[1:2]
    return cosine[0:1] * across, sine[0:1] * across, sine[1:2]


def cell_rows(cell, rows):
    faces = cell.shape[1]
    at = lax.broadcasted_iota(jnp.int32, (rows, faces), 0)
    return jnp.where(at == cell // 16, 1.0, 0.0).astype(jnp.bfloat16)


def cell_depth(cell, per_brick):
    position = lax.broadcasted_iota(jnp.int32, cell.shape, 1)
    return position // per_brick * 16 + cell % 16


def face_weight(counts, area, per_brick):
    position = lax.broadcasted_iota(jnp.int32, area.shape, 1)
    brick = position // per_brick
    limit = jnp.zeros(area.shape, jnp.int32)
    for b in range(counts.shape[0]):
        limit = jnp.where(brick == b, counts[b], limit)
    return jnp.where(position % per_brick < limit, area, 0.0)


def turn(jac, direction, values):
    out = []
    for c in range(5):
        total = jac[direction, 0, c] * values[0]
        for k in range(1, 5):
            total = total + jac[direction, k, c] * values[k]
        out.append(total)
    return out


def coupled(jac, direction, side, speed, damping, values):
    factor = relax_factor(damping)
    scaled = (0.5 * side) * factor * speed
    spread = factor * damping
    turned = turn(jac, direction, values)
    return [scaled * turned[c] + spread * values[c] for c in range(5)]


def relax_row(jac, here, x_low, x_high, edge_low, edge_high, source, speed, damping, wall):
    rows, lanes = here[0].shape
    at_y = lax.broadcasted_iota(jnp.int32, (rows, lanes), 0)
    at_z = lax.broadcasted_iota(jnp.int32, (rows, lanes), 1)
    total = [None] * 5
    beside = [None] * 5
    for direction in range(3):
        jumps = []
        for c in range(5):
            if direction == 0:
                low, high = x_low[c], x_high[c]
            elif direction == 1:
                low = jnp.where(at_y == 0, edge_low[c], pltpu.roll(here[c], 1, 0))
                high = jnp.where(at_y == rows - 1, edge_high[c], pltpu.roll(here[c], rows - 1, 0))
            else:
                low = jnp.where(at_z == 0, 0.0, pltpu.roll(here[c], 1, 1))
                high = jnp.where(at_z == lanes - 1, 0.0, pltpu.roll(here[c], lanes - 1, 1))
            both = low + high
            beside[c] = both if beside[c] is None else beside[c] + both
            jumps.append(high - low)
        turned = turn(jac, direction, jumps)
        half = 0.5 * speed[direction]
        for c in range(5):
            part = half * turned[c]
            total[c] = part if total[c] is None else total[c] + part
    factor = relax_factor(damping)
    out = []
    for c in range(5):
        applied = total[c] + damping * (6.0 * here[c] - beside[c])
        if 1 <= c <= 3:
            for d in range(3):
                applied = applied + wall[c - 1][d] * here[1 + d]
        out.append(here[c] + factor * (source[c] - applied))
    return out


SYM = ((0, 1, 2), (1, 3, 4), (2, 4, 5))


def first_kernel(per_brick, jac, counts, cell_ref, angle_ref, area_ref, adjoint, source, velocity, dissip,
                 partial, walls, low_out, high_out):
    faces = cell_ref.shape[0]
    size_x, size_y, size_z = dissip.shape
    cell = cell_ref[...].reshape(1, faces)
    area = area_ref[...].reshape(1, faces)
    normal = face_normals(angle_ref[...])
    weight = face_weight(counts, area, per_brick)
    rows = cell_rows(cell, size_x * size_y)
    depth = cell_depth(cell, per_brick)
    at = lax.broadcasted_iota(jnp.int32, (size_z, faces), 0) == depth
    pairs = ((0, 0), (0, 1), (0, 2), (1, 1), (1, 2), (2, 2))
    for m, (a, b) in enumerate(pairs):
        value = weight * normal[a] * normal[b]
        high, low = halves(value)
        put_high = jnp.where(at, high.astype(jnp.float32), 0.0).astype(jnp.bfloat16)
        put_low = jnp.where(at, low.astype(jnp.float32), 0.0).astype(jnp.bfloat16)
        total = dot_last(rows, put_high) + dot_last(rows, put_low)
        walls[m] = total.reshape(size_x, size_y, size_z)

    def step(x, carry):
        here = [adjoint[c, x] for c in range(5)]
        below = jnp.maximum(x - 1, 0)
        above = jnp.minimum(x + 1, size_x - 1)
        has_low = jnp.where(x > 0, 1.0, 0.0)
        has_high = jnp.where(x < size_x - 1, 1.0, 0.0)
        x_low = [adjoint[c, below] * has_low for c in range(5)]
        x_high = [adjoint[c, above] * has_high for c in range(5)]
        zeros = [0.0] * 5
        src = [source[c, x] for c in range(5)]
        speed = [velocity[d, x].astype(jnp.float32) for d in range(3)]
        damping = dissip[x].astype(jnp.float32)
        sym = [walls[m, x] for m in range(6)]
        wall = [[sym[SYM[a][b]] for b in range(3)] for a in range(3)]
        out = relax_row(jac, here, x_low, x_high, zeros, zeros, src, speed, damping, wall)
        for c in range(5):
            partial[c, x] = out[c]
        fields = here + out + [speed[1], damping, speed[0]]
        for f, field in enumerate(fields):
            low_out[f, pl.ds(x, 1), :] = field[0:1]
            high_out[f, pl.ds(x, 1), :] = field[size_y - 1:size_y]
        return carry

    lax.fori_loop(0, size_x, step, 0)


def second_kernel(jac, from_low, from_high, *refs):
    sets, outs = (refs[0:4], refs[4:8]), refs[8:10]
    for (adjoint, partial, velocity, dissip), out, x in zip(sets, outs, (0, 15)):
        rows = adjoint.shape[2]
        speed_x = velocity[0, 0].astype(jnp.float32)
        speed_y = velocity[1, 0].astype(jnp.float32)
        damping = dissip[0].astype(jnp.float32)
        at_y = lax.broadcasted_iota(jnp.int32, speed_x.shape, 0)
        low = [from_low[c, x:x + 1, :] for c in range(5)]
        high = [from_high[c, x:x + 1, :] for c in range(5)]
        add_low = coupled(jac, 1, 1.0, speed_y[0:1], damping[0:1], low)
        add_high = coupled(jac, 1, -1.0, speed_y[rows - 1:rows], damping[rows - 1:rows], high)
        for c in range(5):
            out[c] = adjoint[c, 0]
            fixed = partial[c, 0]
            fixed = fixed + jnp.where(at_y == 0, add_low[c], 0.0)
            fixed = fixed + jnp.where(at_y == rows - 1, add_high[c], 0.0)
            out[5 + c] = fixed
        out[10] = speed_x
        out[11] = damping
        out[12] = jnp.concatenate(low + high + [jnp.zeros((rows - 10, speed_x.shape[1]), jnp.float32)], axis=0)


def third_kernel(per_brick, n_sfc, n_blk, jac, counts, cell_ref, angle_ref, area_ref, pressure_ref, owner_ref, local_ref,
                 partial, walls, source, velocity, dissip, y_own_low, y_own_high, y_low, y_high,
                 x_own_low, x_own_high, x_low, x_high, relaxed, message, field, edge_low, edge_high):
    faces = cell_ref.shape[0]
    size_x, size_y, size_z = dissip.shape
    for c in range(5):
        field[c, 1:1 + size_x] = partial[c]
    grab = lambda ref: [ref[c] for c in range(5)]
    add = coupled(jac, 0, 1.0, x_own_low[10], x_own_low[11], grab(x_low))
    for c in range(5):
        field[c, 1] = field[c, 1] + add[c]
    add = coupled(jac, 0, -1.0, x_own_high[10], x_own_high[11], grab(x_high))
    for c in range(5):
        field[c, size_x] = field[c, size_x] + add[c]
    add_low = coupled(jac, 1, 1.0, y_own_low[10], y_own_low[11], grab(y_low))
    add_high = coupled(jac, 1, -1.0, y_own_high[10], y_own_high[11], grab(y_high))
    for c in range(5):
        for x in range(size_x):
            field[c, 1 + x, 0:1, :] = field[c, 1 + x, 0:1, :] + add_low[c][x:x + 1]
            field[c, 1 + x, size_y - 1:size_y, :] = field[c, 1 + x, size_y - 1:size_y, :] + add_high[c][x:x + 1]
    add = coupled(jac, 0, -1.0, x_low[10], x_low[11], grab(x_own_low))
    for c in range(5):
        field[c, 0] = x_low[5 + c] + add[c]
    add = coupled(jac, 0, 1.0, x_high[10], x_high[11], grab(x_own_high))
    for c in range(5):
        field[c, size_x + 1] = x_high[5 + c] + add[c]
    at_x = lax.broadcasted_iota(jnp.int32, (size_x, size_z), 0)
    for edge, theirs, own, side, corner in ((edge_low, y_low, y_own_low, -1.0, 0), (edge_high, y_high, y_own_high, 1.0, 5)):
        add = coupled(jac, 1, side, theirs[10], theirs[11], grab(own))
        speed = theirs[12]
        damping = theirs[11]
        first = [x_low[12, corner + c:corner + c + 1, :] for c in range(5)]
        last = [x_high[12, corner + c:corner + c + 1, :] for c in range(5)]
        add_first = coupled(jac, 0, 1.0, speed[0:1], damping[0:1], first)
        add_last = coupled(jac, 0, -1.0, speed[size_x - 1:size_x], damping[size_x - 1:size_x], last)
        for c in range(5):
            value = theirs[5 + c] + add[c]
            value = value + jnp.where(at_x == 0, add_first[c], 0.0)
            edge[c] = value + jnp.where(at_x == size_x - 1, add_last[c], 0.0)

    def step(x, carry):
        here = [field[c, x + 1] for c in range(5)]
        below = [field[c, x] for c in range(5)]
        above = [field[c, x + 2] for c in range(5)]
        lows = [edge_low[c, pl.ds(x, 1), :] for c in range(5)]
        highs = [edge_high[c, pl.ds(x, 1), :] for c in range(5)]
        src = [source[c, x] for c in range(5)]
        speed = [velocity[d, x].astype(jnp.float32) for d in range(3)]
        damping = dissip[x].astype(jnp.float32)
        sym = [walls[m, x] for m in range(6)]
        wall = [[sym[SYM[a][b]] for b in range(3)] for a in range(3)]
        out = relax_row(jac, here, below, above, lows, highs, src, speed, damping, wall)
        for c in range(5):
            relaxed[c, x] = out[c]
        return carry

    lax.fori_loop(0, size_x, step, 0)

    cell = cell_ref[...].reshape(1, faces)
    area = area_ref[...].reshape(1, faces)
    normal = face_normals(angle_ref[...])
    weight = face_weight(counts, area, per_brick)
    rows = cell_rows(cell, size_x * size_y)
    depth = cell_depth(cell, per_brick)
    along = jnp.zeros((size_z, faces), jnp.float32)
    for c in range(3):
        turned = relaxed[1 + c].reshape(size_x * size_y, size_z).T
        high, low = halves(turned)
        picked = lax.dot_general(high, rows, (((1,), (0,)), ((), ())), preferred_element_type=jnp.float32)
        picked = picked + lax.dot_general(low, rows, (((1,), (0,)), ((), ())), preferred_element_type=jnp.float32)
        along = along + normal[c] * picked
    at = lax.broadcasted_iota(jnp.int32, (size_z, faces), 0) == depth
    project = jnp.sum(jnp.where(at, along, 0.0), axis=0, keepdims=True)
    scale = pressure_ref[...].reshape(1, faces) * weight * project
    owner = owner_ref[...].reshape(1, faces)
    label = local_ref[...].reshape(1, faces).astype(jnp.float32)
    block = min(faces, 128)
    number = owner.astype(jnp.float32)
    columns = [jnp.broadcast_to(number[:, t:t + block], (block, block)).T for t in range(0, faces, block)]
    before = (lax.broadcasted_iota(jnp.int32, (block, block), 0)
              < lax.broadcasted_iota(jnp.int32, (block, block), 1))
    ranks = []
    for u in range(faces // block):
        mine = number[:, u * block:(u + 1) * block]
        same = jnp.where((columns[u] == mine) & before, 1.0, 0.0)
        for t in range(u):
            same = same + jnp.where(columns[t] == mine, 1.0, 0.0)
        ranks.append(jnp.sum(same, axis=0, keepdims=True))
    rank = jnp.concatenate(ranks, axis=1)
    words = [normal[0] * scale, normal[1] * scale, normal[2] * scale, label]
    at_blk = owner % n_blk
    entries = []
    for b in range(n_blk):
        for j in range(2):
            keep = (at_blk == b) & (rank == float(j))
            entries += [jnp.where(keep, w, 0.0) for w in words]
    lanes = message.shape[1]
    entries.append(jnp.zeros((lanes - len(entries), faces), jnp.float32))
    high, low = halves(jnp.concatenate(entries, axis=0))
    target = lax.broadcasted_iota(jnp.int32, (n_sfc, faces), 0)
    target = jnp.where(target == owner // n_blk, 1.0, 0.0).astype(jnp.bfloat16)
    message[...] = dot_last(target, high) + dot_last(target, low)


def turn_kernel(words, got, out):
    out[...] = got[...].T[0:words]


def last_kernel(got, out):
    rows, lanes = got.shape
    tris = out.shape[1]
    at = lax.broadcasted_iota(jnp.int32, (tris, lanes), 0).astype(jnp.float32)
    total = jnp.zeros((16, tris), jnp.float32)
    for r in range(0, rows, 4):
        high, low = halves(got[r:r + 4, :])
        both = jnp.concatenate([high.astype(jnp.float32), jnp.zeros((4, lanes), jnp.float32), low.astype(jnp.float32), jnp.zeros((4, lanes), jnp.float32)], axis=0)
        hot = jnp.where(at == got[r + 3:r + 4, :], 1.0, 0.0).astype(jnp.bfloat16)
        total = total + dot_last(both.astype(jnp.bfloat16), hot)
    out[...] = total[0:3] + total[8:11]


def shift_both(axis, low, high):
    count = lax.axis_size(axis)
    forward = [(i, i + 1) for i in range(count - 1)]
    backward = [(j, i) for i, j in forward]
    return lax.ppermute(high, axis, forward), lax.ppermute(low, axis, backward)


def on_device(adjoint, source, velocity, dissip, jacobian, cut_counts, cut_cell, face_angles, face_area, face_pressure,
              tri_owner, tri_local):
    n_sfc, n_blk = lax.axis_size("sfc"), lax.axis_size("blk")
    _, size_x, size_y, size_z = adjoint.shape
    faces = cut_cell.shape[0]
    per_brick = faces // cut_counts.shape[0]
    f32 = jnp.float32
    smem = pl.BlockSpec(memory_space=pltpu.SMEM)
    vmem = pl.BlockSpec(memory_space=pltpu.VMEM)
    shape = jax.ShapeDtypeStruct
    owner = tri_owner.reshape(faces)

    strip = shape((13, 16, size_z), f32)
    partial, walls, y_low_out, y_high_out = pl.pallas_call(
        functools.partial(first_kernel, per_brick),
        in_specs=[smem, smem] + [vmem] * 7,
        out_specs=[vmem] * 4,
        out_shape=[shape(adjoint.shape, f32), shape((6, size_x, size_y, size_z), f32), strip, strip],
        compiler_params=BIG,
        name="first_step",
    )(jacobian, cut_counts, cut_cell, face_angles, face_area, adjoint, source, velocity, dissip)
    from_low, from_high = shift_both("blk", y_low_out, y_high_out)

    def rows_at(x):
        return [pl.BlockSpec((5, 1, size_y, size_z), lambda i: (0, x, 0, 0)),
                pl.BlockSpec((5, 1, size_y, size_z), lambda i: (0, x, 0, 0)),
                pl.BlockSpec((3, 1, size_y, size_z), lambda i: (0, x, 0, 0)),
                pl.BlockSpec((1, size_y, size_z), lambda i: (x, 0, 0))]

    whole = pl.BlockSpec((13, 16, size_z), lambda i: (0, 0, 0))
    x_low_out, x_high_out = pl.pallas_call(
        second_kernel,
        grid=(1,),
        in_specs=[smem, whole, whole] + rows_at(0) + rows_at(size_x - 1),
        out_specs=[whole, whole],
        out_shape=[strip, strip],
        name="edge_rows",
    )(jacobian, from_low, from_high, *([adjoint, partial, velocity, dissip] * 2))
    x_low, x_high = shift_both("sfc", x_low_out, x_high_out)

    relaxed, message = pl.pallas_call(
        functools.partial(third_kernel, per_brick, n_sfc, n_blk),
        in_specs=[smem, smem] + [vmem] * 19,
        out_specs=[vmem] * 2,
        out_shape=[shape(adjoint.shape, f32), shape((n_sfc, 128), f32)],
        scratch_shapes=[pltpu.VMEM((5, size_x + 2, size_y, size_z), f32),
                        pltpu.VMEM((5, size_x, size_z), f32), pltpu.VMEM((5, size_x, size_z), f32)],
        compiler_params=BIG,
        name="second_step",
    )(jacobian, cut_counts, cut_cell, face_angles, face_area, face_pressure, owner, tri_local,
      partial, walls, source, velocity, dissip, y_low_out, y_high_out, from_low, from_high,
      x_low_out, x_high_out, x_low, x_high)

    got = lax.all_to_all(message, "sfc", split_axis=0, concat_axis=0, tiled=True)
    words = 8 * n_blk
    turned = pl.pallas_call(
        functools.partial(turn_kernel, words),
        in_specs=[vmem],
        out_specs=vmem,
        out_shape=shape((words, n_sfc), f32),
        name="turn_words",
    )(got)
    got = lax.all_to_all(turned, "blk", split_axis=0, concat_axis=0, tiled=True)
    sensitivity = pl.pallas_call(
        last_kernel,
        in_specs=[vmem],
        out_specs=vmem,
        out_shape=shape((3, TRI_DEV), f32),
        name="sum_terms",
    )(got)
    return relaxed, sensitivity


def solution(mesh):
    return jax.shard_map(
        on_device,
        mesh=mesh,
        in_specs=(
            P(None, "sfc", "blk", None),
            P(None, "sfc", "blk", None),
            P(None, "sfc", "blk", None),
            P("sfc", "blk", None),
            P(),
            P(("sfc", "blk")),
            P(("sfc", "blk")),
            P(None, ("sfc", "blk")),
            P(("sfc", "blk")),
            P(("sfc", "blk")),
            P(("sfc", "blk"), None),
            P(("sfc", "blk")),
        ),
        out_specs=(P(None, "sfc", "blk", None), P(None, ("sfc", "blk"))),
        check_vma=False,
    )
```

```python
import functools

import jax
import jax.numpy as jnp
from jax import lax
from jax.experimental import pallas as pl
from jax.experimental.pallas import tpu as pltpu
from jax.sharding import PartitionSpec as P

TRI_DEV = 256
OMEGA = 0.8
ROOM = pltpu.CompilerParams(vmem_limit_bytes=20 * 1024 * 1024)

SMALL = pltpu.CompilerParams(vmem_limit_bytes=4 * 1024 * 1024)


def dot_last(a, b):
    return lax.dot_general(a, b, (((1,), (1,)), ((), ())), preferred_element_type=jnp.float32)


def halves(x):
    high = x.astype(jnp.bfloat16)
    return high, (x - high.astype(jnp.float32)).astype(jnp.bfloat16)


def relax_factor(damping):
    return OMEGA / (6.0 * damping + 1.0)


def face_normals(angles):
    cosine = jnp.cos(angles)
    sine = jnp.sin(angles)
    across = cosine[1:2]
    return cosine[0:1] * across, sine[0:1] * across, sine[1:2]


def cell_rows(cell, rows):
    faces = cell.shape[1]
    at = lax.broadcasted_iota(jnp.int32, (rows, faces), 0)
    return jnp.where(at == cell // 16, 1.0, 0.0).astype(jnp.bfloat16)


def cell_depth(cell, per_brick):
    position = lax.broadcasted_iota(jnp.int32, cell.shape, 1)
    return position // per_brick * 16 + cell % 16


def face_weight(counts, area, per_brick):
    position = lax.broadcasted_iota(jnp.int32, area.shape, 1)
    brick = position // per_brick
    limit = jnp.zeros(area.shape, jnp.int32)
    for b in range(counts.shape[0]):
        limit = jnp.where(brick == b, counts[b], limit)
    return jnp.where(position % per_brick < limit, area, 0.0)


def turn(jac, direction, values):
    out = []
    for c in range(5):
        total = jac[0, direction, c] * values[0]
        for k in range(1, 5):
            total = total + jac[k, direction, c] * values[k]
        out.append(total)
    return out


def coupled(jac, direction, side, speed, damping, values):
    factor = relax_factor(damping)
    scaled = (0.5 * side) * factor * speed
    spread = factor * damping
    turned = turn(jac, direction, values)
    return [scaled * turned[c] + spread * values[c] for c in range(5)]


def relax_row(jac, here, x_low, x_high, edge_low, edge_high, source, speed, damping, wall):
    rows, lanes = here[0].shape
    at_y = lax.broadcasted_iota(jnp.int32, (rows, lanes), 0)
    at_z = lax.broadcasted_iota(jnp.int32, (rows, lanes), 1)
    total = [None] * 5
    beside = [None] * 5
    for direction in range(3):
        jumps = []
        for c in range(5):
            if direction == 0:
                low, high = x_low[c], x_high[c]
            elif direction == 1:
                low = jnp.where(at_y == 0, edge_low[c], pltpu.roll(here[c], 1, 0))
                high = jnp.where(at_y == rows - 1, edge_high[c], pltpu.roll(here[c], rows - 1, 0))
            else:
                low = jnp.where(at_z == 0, 0.0, pltpu.roll(here[c], 1, 1))
                high = jnp.where(at_z == lanes - 1, 0.0, pltpu.roll(here[c], lanes - 1, 1))
            both = low + high
            beside[c] = both if beside[c] is None else beside[c] + both
            jumps.append(high - low)
        turned = turn(jac, direction, jumps)
        half = 0.5 * speed[direction]
        for c in range(5):
            part = half * turned[c]
            total[c] = part if total[c] is None else total[c] + part
    factor = relax_factor(damping)
    out = []
    for c in range(5):
        applied = total[c] + damping * (6.0 * here[c] - beside[c])
        if 1 <= c <= 3:
            for d in range(3):
                applied = applied + wall[c - 1][d] * here[1 + d]
        out.append(here[c] + factor * (source[c] - applied))
    return out


SYM = ((0, 1, 2), (1, 3, 4), (2, 4, 5))


def start_all(pairs, sems):
    copies = [pltpu.make_async_copy(src, dst, sems.at[i]) for i, (src, dst) in enumerate(pairs)]
    for copy in copies:
        copy.start()
    return copies


def wait_all(copies):
    for copy in copies:
        copy.wait()


def first_kernel(per_brick, jac, counts, cell_hbm, angle_hbm, area_hbm, adjoint_hbm, source_hbm, velocity_hbm, dissip_hbm,
                 partial, walls, near_out, far_out, first_out, last_out,
                 cell_ref, angle_ref, area_ref, field, source, velocity, dissip, edges, sems):
    size_x, size_y, size_z = dissip.shape
    copies = start_all([(cell_hbm, cell_ref), (angle_hbm, angle_ref), (area_hbm, area_ref),
                        (adjoint_hbm, field.at[:, pl.ds(1, size_x)]), (velocity_hbm, velocity),
                        (dissip_hbm, dissip), (source_hbm, source)], sems)
    side = 1 - lax.axis_index("blk") % 2
    faces = cell_ref.shape[0]
    blank = jnp.zeros((size_y, size_z), jnp.float32)
    for c in range(5):
        field[c, 0] = blank
        field[c, size_x + 1] = blank
    wait_all(copies[:3])
    cell = cell_ref[...].reshape(1, faces)
    area = area_ref[...].reshape(1, faces)
    normal = face_normals(angle_ref[...])
    weight = face_weight(counts, area, per_brick)
    rows = cell_rows(cell, size_x * size_y)
    depth = cell_depth(cell, per_brick)
    at = lax.broadcasted_iota(jnp.int32, (size_z, faces), 0) == depth
    hot = jnp.where(at, 1.0, 0.0).astype(jnp.bfloat16)
    rows = jnp.concatenate([rows, rows], axis=1)
    pairs = ((0, 0), (0, 1), (0, 2), (1, 1), (1, 2), (2, 2))
    for m in range(0, 6, 2):
        put = []
        for a, b in pairs[m:m + 2]:
            high, low = halves(weight * normal[a] * normal[b])
            put.append(jnp.concatenate([hot * high, hot * low], axis=1))
        total = dot_last(rows, jnp.concatenate(put, axis=0))
        walls[m] = total[:, :size_z].reshape(size_x, size_y, size_z)
        walls[m + 1] = total[:, size_z:].reshape(size_x, size_y, size_z)
    wait_all(copies[3:])

    def step(x, carry):
        here = [field[c, x + 1] for c in range(5)]
        below = [field[c, x] for c in range(5)]
        above = [field[c, x + 2] for c in range(5)]
        zeros = [0.0] * 5
        src = [source[c, x] for c in range(5)]
        speed = [velocity[d, x].astype(jnp.float32) for d in range(3)]
        damping = dissip[x].astype(jnp.float32)
        sym = [walls[m, x] for m in range(6)]
        wall = [[sym[SYM[a][b]] for b in range(3)] for a in range(3)]
        out = relax_row(jac, here, below, above, zeros, zeros, src, speed, damping, wall)
        for c in range(5):
            partial[c, x] = out[c]
        fields = here + out + [speed[1], damping, speed[0]]
        for f, edge in enumerate(fields):
            edges[side, f, pl.ds(x, 1), :] = edge[0:1]
            edges[1 - side, f, pl.ds(x, 1), :] = edge[size_y - 1:size_y]
        return carry

    lax.fori_loop(0, size_x, step, 0, unroll=2)
    near_out[...] = edges[0]
    far_out[...] = edges[1]
    for out, x in ((first_out, 0), (last_out, size_x - 1)):
        for c in range(5):
            out[c] = field[c, x + 1]
            out[5 + c] = partial[c, x]
        out[10] = velocity[0, x].astype(jnp.float32)
        out[11] = dissip[x].astype(jnp.float32)
        out[12] = velocity[1, x].astype(jnp.float32)


def second_kernel(jac, from_near, from_far, first, last, near_out, far_out, both):
    rows, lanes = first.shape[1:]
    at_y = lax.broadcasted_iota(jnp.int32, (rows, lanes), 0)
    odd = lax.axis_index("blk") % 2 == 1
    side = 1 - lax.axis_index("core")
    for mine, place, x in ((first, side, 0), (last, 1 - side, from_near.shape[1] - 1)):
        speed_y = mine[12]
        damping = mine[11]
        near = [from_near[c, x:x + 1, :] for c in range(5)]
        far = [from_far[c, x:x + 1, :] for c in range(5)]
        low = [jnp.where(odd, a, b) for a, b in zip(near, far)]
        high = [jnp.where(odd, b, a) for a, b in zip(near, far)]
        add_low = coupled(jac, 1, 1.0, speed_y[0:1], damping[0:1], low)
        add_high = coupled(jac, 1, -1.0, speed_y[rows - 1:rows], damping[rows - 1:rows], high)
        for c in range(5):
            both[place, c] = mine[c]
            fixed = mine[5 + c]
            fixed = fixed + jnp.where(at_y == 0, add_low[c], 0.0)
            both[place, 5 + c] = fixed + jnp.where(at_y == rows - 1, add_high[c], 0.0)
        both[place, 10] = mine[10]
        both[place, 11] = damping
        both[place, 12] = jnp.concatenate(low + high + [jnp.zeros((rows - 10, lanes), jnp.float32)], axis=0)
    near_out[...] = both[0]
    far_out[...] = both[1]


def third_kernel(per_brick, parts, jac, counts, cell_ref, angle_ref, area_ref, pressure_ref, owner_hbm, local_ref,
                 partial, walls, source_hbm, velocity_hbm, dissip_hbm, y_own_near, y_own_far, y_near, y_far,
                 x_own_near, x_own_far, x_near, x_far, relaxed_hbm, message,
                 field, edge_low, edge_high, relaxed, source, velocity, dissip, owner_ref, sems, out_sem):
    copies = start_all([(velocity_hbm, velocity), (dissip_hbm, dissip), (source_hbm, source), (owner_hbm, owner_ref)], sems)
    faces = cell_ref.shape[0]
    size_x, size_y, size_z = dissip.shape
    for c in range(5):
        field[c, 1:1 + size_x] = partial[c]
    odd_y = lax.axis_index("blk") % 2 == 1
    odd_x = lax.axis_index("core") == 1

    class Sorted:
        def __init__(self, odd, when_odd, when_even):
            self.odd, self.when_odd, self.when_even = odd, when_odd, when_even

        def __getitem__(self, at):
            return jnp.where(self.odd, self.when_odd[at], self.when_even[at])

    y_low, y_high = Sorted(odd_y, y_near, y_far), Sorted(odd_y, y_far, y_near)
    y_own_low, y_own_high = Sorted(odd_y, y_own_near, y_own_far), Sorted(odd_y, y_own_far, y_own_near)
    x_low, x_high = Sorted(odd_x, x_near, x_far), Sorted(odd_x, x_far, x_near)
    x_own_low, x_own_high = Sorted(odd_x, x_own_near, x_own_far), Sorted(odd_x, x_own_far, x_own_near)
    grab = lambda ref: [ref[c] for c in range(5)]
    add = coupled(jac, 0, 1.0, x_own_low[10], x_own_low[11], grab(x_low))
    for c in range(5):
        field[c, 1] = field[c, 1] + add[c]
    add = coupled(jac, 0, -1.0, x_own_high[10], x_own_high[11], grab(x_high))
    for c in range(5):
        field[c, size_x] = field[c, size_x] + add[c]
    add_low = coupled(jac, 1, 1.0, y_own_low[10], y_own_low[11], grab(y_low))
    add_high = coupled(jac, 1, -1.0, y_own_high[10], y_own_high[11], grab(y_high))
    for c in range(5):
        for x in range(size_x):
            field[c, 1 + x, 0:1, :] = field[c, 1 + x, 0:1, :] + add_low[c][x:x + 1]
            field[c, 1 + x, size_y - 1:size_y, :] = field[c, 1 + x, size_y - 1:size_y, :] + add_high[c][x:x + 1]
    add = coupled(jac, 0, -1.0, x_low[10], x_low[11], grab(x_own_low))
    for c in range(5):
        field[c, 0] = x_low[5 + c] + add[c]
    add = coupled(jac, 0, 1.0, x_high[10], x_high[11], grab(x_own_high))
    for c in range(5):
        field[c, size_x + 1] = x_high[5 + c] + add[c]
    at_x = lax.broadcasted_iota(jnp.int32, (size_x, size_z), 0)
    for edge, theirs, own, side, corner in ((edge_low, y_low, y_own_low, -1.0, 0), (edge_high, y_high, y_own_high, 1.0, 5)):
        add = coupled(jac, 1, side, theirs[10], theirs[11], grab(own))
        speed = theirs[12]
        damping = theirs[11]
        first = [x_low[12, corner + c:corner + c + 1, :] for c in range(5)]
        last = [x_high[12, corner + c:corner + c + 1, :] for c in range(5)]
        add_first = coupled(jac, 0, 1.0, speed[0:1], damping[0:1], first)
        add_last = coupled(jac, 0, -1.0, speed[size_x - 1:size_x], damping[size_x - 1:size_x], last)
        for c in range(5):
            value = theirs[5 + c] + add[c]
            value = value + jnp.where(at_x == 0, add_first[c], 0.0)
            edge[c] = value + jnp.where(at_x == size_x - 1, add_last[c], 0.0)

    def step(x, carry):
        here = [field[c, x + 1] for c in range(5)]
        below = [field[c, x] for c in range(5)]
        above = [field[c, x + 2] for c in range(5)]
        lows = [edge_low[c, pl.ds(x, 1), :] for c in range(5)]
        highs = [edge_high[c, pl.ds(x, 1), :] for c in range(5)]
        src = [source[c, x] for c in range(5)]
        speed = [velocity[d, x].astype(jnp.float32) for d in range(3)]
        damping = dissip[x].astype(jnp.float32)
        sym = [walls[m, x] for m in range(6)]
        wall = [[sym[SYM[a][b]] for b in range(3)] for a in range(3)]
        out = relax_row(jac, here, below, above, lows, highs, src, speed, damping, wall)
        for c in range(5):
            relaxed[c, x] = out[c]
        return carry

    wait_all(copies)
    lax.fori_loop(0, size_x, step, 0, unroll=2)
    done = pltpu.make_async_copy(relaxed, relaxed_hbm, out_sem)
    done.start()

    cell = cell_ref[...].reshape(1, faces)
    area = area_ref[...].reshape(1, faces)
    normal = face_normals(angle_ref[...])
    weight = face_weight(counts, area, per_brick)
    rows = cell_rows(cell, size_x * size_y)
    depth = cell_depth(cell, per_brick)
    turned = []
    for c in range(3):
        high, low = halves(relaxed[1 + c].reshape(size_x * size_y, size_z).T)
        turned.append(jnp.concatenate([high, low], axis=1))
    picked = jnp.dot(jnp.concatenate(turned, axis=0), jnp.concatenate([rows, rows], axis=0),
                     preferred_element_type=jnp.float32)
    along = normal[0] * picked[:size_z] + normal[1] * picked[size_z:2 * size_z] + normal[2] * picked[2 * size_z:]
    at = lax.broadcasted_iota(jnp.int32, (size_z, faces), 0) == depth
    project = jnp.sum(jnp.where(at, along, 0.0), axis=0, keepdims=True)
    scale = pressure_ref[...].reshape(1, faces) * weight * project
    owner = owner_ref[...].reshape(1, faces)
    label = local_ref[...].reshape(1, faces).astype(jnp.float32)
    block = min(faces, 128)
    number = owner.astype(jnp.float32)
    columns = [jnp.broadcast_to(number[:, t:t + block], (block, block)).T for t in range(0, faces, block)]
    before = (lax.broadcasted_iota(jnp.int32, (block, block), 0)
              < lax.broadcasted_iota(jnp.int32, (block, block), 1))
    ranks = []
    for u in range(faces // block):
        mine = number[:, u * block:(u + 1) * block]
        same = jnp.where((columns[u] == mine) & before, 1.0, 0.0)
        for t in range(u):
            same = same + jnp.where(columns[t] == mine, 1.0, 0.0)
        ranks.append(jnp.sum(same, axis=0, keepdims=True))
    rank = jnp.concatenate(ranks, axis=1)
    n_y, n_z, n_c, n_x = parts
    words = [normal[0] * scale, normal[1] * scale, normal[2] * scale, label]
    pair = [jnp.where(rank == float(j), w, 0.0) for j in range(2) for w in words]
    high, low = halves(jnp.concatenate(pair * n_z, axis=0))
    at_x, at_c, at_z, at_y = owner % n_x, owner // n_x % n_c, owner // (n_x * n_c) % n_z, owner // (n_x * n_c * n_z)
    lane = lax.broadcasted_iota(jnp.int32, (8 * n_z, faces), 0)
    hot = jnp.where(lane // 8 == at_z, 1.0, 0.0).astype(jnp.bfloat16)
    target = lax.broadcasted_iota(jnp.int32, (n_y * n_c * n_x, faces), 0)
    target = jnp.where(target == (at_y * n_c + at_c) * n_x + at_x, 1.0, 0.0).astype(jnp.bfloat16)
    message[...] = dot_last(jnp.concatenate([target, target], axis=1),
                            jnp.concatenate([hot * high, hot * low], axis=1))
    done.wait()


def turn_kernel(got, out):
    turned = got[...].T
    blank = jnp.zeros((turned.shape[0], out.shape[1] - turned.shape[1]), jnp.float32)
    out[...] = jnp.concatenate([turned, blank], axis=1)


def last_kernel(used, got, out):
    tris = out.shape[1]
    rows = got.shape[0]
    fold = max(1, min(128 // used, rows // 8))
    rows = rows // fold
    packed = jnp.concatenate([got[g * rows:(g + 1) * rows, 0:used] for g in range(fold)], axis=1)
    at = lax.broadcasted_iota(jnp.int32, (tris, fold * used), 0).astype(jnp.float32)
    values, hot = [], []
    for r in range(0, rows, 8):
        tile = packed[r:r + 8]
        for j in range(2):
            high, low = halves(tile if j == 0 else pltpu.roll(tile, 4, 0))
            both = jnp.concatenate([high.astype(jnp.float32), low.astype(jnp.float32)], axis=0)
            values.append(both.astype(jnp.bfloat16))
            hot.append(jnp.where(at == tile[4 * j + 3:4 * j + 4], 1.0, 0.0).astype(jnp.bfloat16))
    total = dot_last(jnp.concatenate(values, axis=1), jnp.concatenate(hot, axis=1))
    out[...] = total[0:3] + total[8:11]


def swap(axis, near, far):
    count = lax.axis_size(axis)
    inside = [(i, i ^ 1) for i in range(count)]
    across = [(i, i + 1 if i % 2 else i - 1) for i in range(1, count - 1)]
    from_far = lax.ppermute(far, axis, across)
    return lax.ppermute(near, axis, inside), from_far


SFC = ("y", "z", "core")


def on_device(adjoint, source, velocity, dissip, jacobian, cut_counts, cut_cell, face_angles, face_area, face_pressure,
              tri_owner, tri_local):
    parts = tuple(lax.axis_size(a) for a in SFC + ("blk",))
    n_y, n_z, n_c, n_x = parts
    _, size_x, size_y, size_z = adjoint.shape
    faces = cut_cell.shape[0]
    per_brick = faces // cut_counts.shape[0]
    f32 = jnp.float32
    smem = pl.BlockSpec(memory_space=pltpu.SMEM)
    vmem = pl.BlockSpec(memory_space=pltpu.VMEM)
    hbm = pl.BlockSpec(memory_space=pltpu.HBM)
    shape = jax.ShapeDtypeStruct
    owner = tri_owner.reshape(faces)
    jacobian = jnp.transpose(jacobian, (1, 0, 2))

    strip = shape((13, 16, size_z), f32)
    block = shape(adjoint.shape, f32)
    wall = shape((6, size_x, size_y, size_z), f32)
    dma = pltpu.SemaphoreType.DMA
    scratch = lambda *arrays: [pltpu.VMEM(a.shape, a.dtype) for a in arrays]
    padded = shape((5, size_x + 2, size_y, size_z), f32)
    edge = shape((5, size_x, size_z), f32)
    far_memory = lambda *arrays: [pltpu.with_memory_space_constraint(a, pltpu.HBM) for a in arrays]
    partial, walls, y_near_out, y_far_out, first, last = pl.pallas_call(
        functools.partial(first_kernel, per_brick),
        in_specs=[smem, smem] + [hbm] * 7,
        out_specs=[vmem] * 6,
        out_shape=[block, wall] + [strip] * 4,
        scratch_shapes=scratch(cut_cell, face_angles, face_area, padded, source, velocity, dissip)
        + [pltpu.VMEM((2,) + strip.shape, f32), dma((7,))],
        compiler_params=ROOM,
        name="first_step",
    )(jacobian, cut_counts, *far_memory(cut_cell, face_angles, face_area, adjoint, source, velocity, dissip))
    from_near, from_far = swap("blk", y_near_out, y_far_out)

    x_near_out, x_far_out = pl.pallas_call(
        second_kernel,
        in_specs=[smem] + [vmem] * 4,
        out_specs=[vmem] * 2,
        out_shape=[strip, strip],
        scratch_shapes=[pltpu.VMEM((2,) + strip.shape, f32)],
        compiler_params=SMALL,
        name="edge_rows",
    )(jacobian, from_near, from_far, first, last)
    x_near, x_far = swap(SFC, x_near_out, x_far_out)

    relaxed, message = pl.pallas_call(
        functools.partial(third_kernel, per_brick, parts),
        in_specs=[smem, smem] + [vmem] * 4 + [hbm] + [vmem] * 3 + [hbm] * 3 + [vmem] * 8,
        out_specs=[hbm, vmem],
        out_shape=[block, shape((n_y * n_c * n_x, 8 * n_z), f32)],
        scratch_shapes=scratch(padded, edge, edge, block, source, velocity, dissip, owner) + [dma((4,)), dma],
        compiler_params=ROOM,
        name="second_step",
    )(jacobian, cut_counts, cut_cell, face_angles, face_area, face_pressure, *far_memory(owner), tri_local, partial, walls,
      *far_memory(source, velocity, dissip), y_near_out, y_far_out, from_near, from_far, x_near_out, x_far_out, x_near, x_far)

    got = lax.all_to_all(message, ("y", "core", "blk"), split_axis=0, concat_axis=0, tiled=True)
    turned = pl.pallas_call(
        turn_kernel,
        in_specs=[vmem],
        out_specs=vmem,
        out_shape=shape((8 * n_z, 128), f32),
        compiler_params=SMALL,
        name="turn_words",
    )(got)
    got = lax.all_to_all(turned, "z", split_axis=0, concat_axis=0, tiled=True)
    sensitivity = pl.pallas_call(
        functools.partial(last_kernel, n_y * n_c * n_x),
        in_specs=[vmem],
        out_specs=vmem,
        out_shape=shape((3, TRI_DEV), f32),
        compiler_params=SMALL,
        name="sum_terms",
    )(got)
    return relaxed, sensitivity


def solution(mesh):
    n_sfc, n_blk = mesh.shape["sfc"], mesh.shape["blk"]
    n_z = min(16, n_sfc // 2)
    split = jax.sharding.Mesh(mesh.devices.reshape(n_sfc // (2 * n_z), n_z, 2, n_blk), SFC + ("blk",))
    grid = P(None, SFC, "blk", None)
    both = SFC + ("blk",)
    return jax.shard_map(
        on_device,
        mesh=split,
        in_specs=(grid, grid, grid, P(SFC, "blk", None), P(), P(both), P(both), P(None, both), P(both), P(both),
                  P(both, None), P(both)),
        out_specs=(grid, P(None, both)),
        check_vma=False,
    )
```

```python
import functools

import jax
import jax.numpy as jnp
from jax import lax
from jax.experimental import pallas as pl
from jax.experimental.pallas import tpu as pltpu
from jax.sharding import PartitionSpec as P

TRI_DEV = 256
OMEGA = 0.8
ROOM = pltpu.CompilerParams(vmem_limit_bytes=20 * 1024 * 1024)

SMALL = pltpu.CompilerParams(vmem_limit_bytes=4 * 1024 * 1024)


def dot_last(a, b):
    return lax.dot_general(a, b, (((1,), (1,)), ((), ())), preferred_element_type=jnp.float32)


def halves(x):
    high = x.astype(jnp.bfloat16)
    return high, (x - high.astype(jnp.float32)).astype(jnp.bfloat16)


def relax_factor(damping):
    return OMEGA / (6.0 * damping + 1.0)


def face_normals(angles):
    cosine = jnp.cos(angles)
    sine = jnp.sin(angles)
    across = cosine[1:2]
    return cosine[0:1] * across, sine[0:1] * across, sine[1:2]


def one_hot(index, size):
    at = lax.broadcasted_iota(jnp.int32, (size, index.shape[1]), 0)
    return jnp.where(at == index, 1.0, 0.0).astype(jnp.bfloat16)


def cell_depth(cell, per_brick):
    position = lax.broadcasted_iota(jnp.int32, cell.shape, 1)
    return position // per_brick * 16 + cell % 16


def face_weight(counts, area, per_brick):
    position = lax.broadcasted_iota(jnp.int32, area.shape, 1)
    brick = position // per_brick
    limit = jnp.zeros(area.shape, jnp.int32)
    for b in range(counts.shape[0]):
        limit = jnp.where(brick == b, counts[b], limit)
    return jnp.where(position % per_brick < limit, area, 0.0)


def turn(jac, direction, values):
    out = []
    for c in range(5):
        total = jac[0, direction, c] * values[0]
        for k in range(1, 5):
            total = total + jac[k, direction, c] * values[k]
        out.append(total)
    return out


def coupled(jac, direction, side, speed, damping, values):
    factor = relax_factor(damping)
    scaled = (0.5 * side) * factor * speed
    spread = factor * damping
    turned = turn(jac, direction, values)
    return [scaled * turned[c] + spread * values[c] for c in range(5)]


def relax_row(jac, here, x_low, x_high, edge_low, edge_high, source, speed, damping, wall):
    rows, lanes = here[0].shape
    at_y = lax.broadcasted_iota(jnp.int32, (rows, lanes), 0)
    at_z = lax.broadcasted_iota(jnp.int32, (rows, lanes), 1)
    total = [None] * 5
    beside = [None] * 5
    for direction in range(3):
        jumps = []
        for c in range(5):
            if direction == 0:
                low, high = x_low[c], x_high[c]
            elif direction == 1:
                low = jnp.where(at_y == 0, edge_low[c], pltpu.roll(here[c], 1, 0))
                high = jnp.where(at_y == rows - 1, edge_high[c], pltpu.roll(here[c], rows - 1, 0))
            else:
                low = jnp.where(at_z == 0, 0.0, pltpu.roll(here[c], 1, 1))
                high = jnp.where(at_z == lanes - 1, 0.0, pltpu.roll(here[c], lanes - 1, 1))
            both = low + high
            beside[c] = both if beside[c] is None else beside[c] + both
            jumps.append(high - low)
        turned = turn(jac, direction, jumps)
        half = 0.5 * speed[direction]
        for c in range(5):
            part = half * turned[c]
            total[c] = part if total[c] is None else total[c] + part
    factor = relax_factor(damping)
    out = []
    for c in range(5):
        applied = total[c] + damping * (6.0 * here[c] - beside[c])
        if 1 <= c <= 3:
            for d in range(3):
                applied = applied + wall[c - 1][d] * here[1 + d]
        out.append(here[c] + factor * (source[c] - applied))
    return out


SYM = ((0, 1, 2), (1, 3, 4), (2, 4, 5))


def start_all(pairs, sems):
    copies = [pltpu.make_async_copy(src, dst, sems.at[i]) for i, (src, dst) in enumerate(pairs)]
    for copy in copies:
        copy.start()
    return copies


def wait_all(copies):
    for copy in copies:
        copy.wait()


def first_kernel(per_brick, jac, counts, cell_hbm, angle_hbm, area_hbm, adjoint_hbm, source_hbm, velocity_hbm, dissip_hbm,
                 partial, walls, near_out, far_out, near_end, far_end, face_out,
                 cell_ref, angle_ref, area_ref, field, source, velocity, dissip, edges, sems):
    size_x, size_y, size_z = dissip.shape
    copies = start_all([(cell_hbm, cell_ref), (angle_hbm, angle_ref), (area_hbm, area_ref),
                        (adjoint_hbm, field.at[:, pl.ds(1, size_x)]), (velocity_hbm, velocity),
                        (dissip_hbm, dissip), (source_hbm, source)], sems)
    side = 1 - lax.axis_index("blk") % 2
    faces = cell_ref.shape[0]
    blank = jnp.zeros((size_y, size_z), jnp.float32)
    for c in range(5):
        field[c, 0] = blank
        field[c, size_x + 1] = blank
    wait_all(copies[:3])
    cell = cell_ref[...].reshape(1, faces)
    area = area_ref[...].reshape(1, faces)
    normal = face_normals(angle_ref[...])
    weight = face_weight(counts, area, per_brick)
    rows = one_hot(cell // 16, size_x * size_y)
    depth = cell_depth(cell, per_brick)
    at = lax.broadcasted_iota(jnp.int32, (size_z, faces), 0) == depth
    hot = jnp.where(at, 1.0, 0.0).astype(jnp.bfloat16)
    face_out[...] = jnp.concatenate([*normal, weight, jnp.zeros((4, faces), jnp.float32)], axis=0)
    rows = jnp.concatenate([rows, rows], axis=1)
    pairs = ((0, 0), (0, 1), (0, 2), (1, 1), (1, 2), (2, 2))
    for m in range(0, 6, 2):
        put = []
        for a, b in pairs[m:m + 2]:
            high, low = halves(weight * normal[a] * normal[b])
            put.append(jnp.concatenate([hot * high, hot * low], axis=1))
        total = dot_last(rows, jnp.concatenate(put, axis=0))
        walls[m] = total[:, :size_z].reshape(size_x, size_y, size_z)
        walls[m + 1] = total[:, size_z:].reshape(size_x, size_y, size_z)
    wait_all(copies[3:])

    def step(x, carry):
        here = [field[c, x + 1] for c in range(5)]
        below = [field[c, x] for c in range(5)]
        above = [field[c, x + 2] for c in range(5)]
        zeros = [0.0] * 5
        src = [source[c, x] for c in range(5)]
        speed = [velocity[d, x].astype(jnp.float32) for d in range(3)]
        damping = dissip[x].astype(jnp.float32)
        sym = [walls[m, x] for m in range(6)]
        wall = [[sym[SYM[a][b]] for b in range(3)] for a in range(3)]
        out = relax_row(jac, here, below, above, zeros, zeros, src, speed, damping, wall)
        for c in range(5):
            partial[c, x] = out[c]
        fields = here + out + [speed[1], damping, speed[0]]
        for f, edge in enumerate(fields):
            edges[side, f, pl.ds(x, 1), :] = edge[0:1]
            edges[1 - side, f, pl.ds(x, 1), :] = edge[size_y - 1:size_y]
        return carry

    lax.fori_loop(0, size_x, step, 0, unroll=2)
    near_out[...] = edges[0]
    far_out[...] = edges[1]
    odd = lax.axis_index("core")
    for out, x in ((near_end, (1 - odd) * (size_x - 1)), (far_end, odd * (size_x - 1))):
        for c in range(5):
            out[c] = field[c, x + 1]
            out[5 + c] = partial[c, x]
        out[10] = velocity[0, x].astype(jnp.float32)
        out[11] = dissip[x].astype(jnp.float32)
        out[12] = velocity[1, x].astype(jnp.float32)


def edge_kernel(is_near, jac, from_near, from_far, mine, out):
    rows, lanes = mine.shape[1:]
    at_y = lax.broadcasted_iota(jnp.int32, (rows, lanes), 0)
    odd_y = lax.axis_index("blk") % 2 == 1
    last = (lax.axis_index("core") == 1) != is_near
    end = from_near.shape[1] - 1
    near = [jnp.where(last, from_near[c, end:end + 1, :], from_near[c, 0:1, :]) for c in range(5)]
    far = [jnp.where(last, from_far[c, end:end + 1, :], from_far[c, 0:1, :]) for c in range(5)]
    low = [jnp.where(odd_y, a, b) for a, b in zip(near, far)]
    high = [jnp.where(odd_y, b, a) for a, b in zip(near, far)]
    speed_y = mine[12]
    damping = mine[11]
    add_low = coupled(jac, 1, 1.0, speed_y[0:1], damping[0:1], low)
    add_high = coupled(jac, 1, -1.0, speed_y[rows - 1:rows], damping[rows - 1:rows], high)
    for c in range(5):
        out[c] = mine[c]
        fixed = mine[5 + c]
        fixed = fixed + jnp.where(at_y == 0, add_low[c], 0.0)
        out[5 + c] = fixed + jnp.where(at_y == rows - 1, add_high[c], 0.0)
    out[10] = mine[10]
    out[11] = damping
    out[12] = jnp.concatenate(low + high + [jnp.zeros((rows - 10, lanes), jnp.float32)], axis=0)


def plan_kernel(per_brick, parts, after, face, cell_ref, pressure_ref, owner_ref, local_ref, plan):
    del after
    faces = cell_ref.shape[0]
    cell = cell_ref[...].reshape(1, faces)
    owner = owner_ref[...].reshape(1, faces)
    strength = pressure_ref[...].reshape(1, faces) * face[3:4]
    label = local_ref[...].reshape(1, faces).astype(jnp.float32)
    block = min(faces, 128)
    number = owner.astype(jnp.float32)
    columns = [jnp.broadcast_to(number[:, t:t + block], (block, block)).T for t in range(0, faces, block)]
    before = (lax.broadcasted_iota(jnp.int32, (block, block), 0)
              < lax.broadcasted_iota(jnp.int32, (block, block), 1))
    ranks = []
    for u in range(faces // block):
        mine = number[:, u * block:(u + 1) * block]
        same = jnp.where((columns[u] == mine) & before, 1.0, 0.0)
        for t in range(u):
            same = same + jnp.where(columns[t] == mine, 1.0, 0.0)
        ranks.append(jnp.sum(same, axis=0, keepdims=True))
    rank = jnp.concatenate(ranks, axis=1)
    n_y, n_z, n_c, n_x = parts
    at_x, at_c, at_z, at_y = owner % n_x, owner // n_x % n_c, owner // (n_x * n_c) % n_z, owner // (n_x * n_c * n_z)
    whole = [cell // 16, cell_depth(cell, per_brick), at_z, (at_y * n_c + at_c) * n_x + at_x]
    rows = [face[0:1], face[1:2], face[2:3], strength, rank, label] + [w.astype(jnp.float32) for w in whole]
    plan[...] = jnp.concatenate(rows + [jnp.zeros((16 - len(rows), faces), jnp.float32)], axis=0)


def third_kernel(parts, jac, plan, partial, walls, source, velocity, dissip, y_own_near, y_own_far, y_near, y_far,
                 x_own_near, x_own_far, x_near, x_far, relaxed_hbm, message,
                 field, edge_low, edge_high, relaxed, out_sem):
    faces = plan.shape[1]
    size_x, size_y, size_z = dissip.shape
    for c in range(5):
        field[c, 1:1 + size_x] = partial[c]
    odd_y = lax.axis_index("blk") % 2 == 1
    odd_x = lax.axis_index("core") == 1

    class Sorted:
        def __init__(self, odd, when_odd, when_even):
            self.odd, self.when_odd, self.when_even = odd, when_odd, when_even

        def __getitem__(self, at):
            return jnp.where(self.odd, self.when_odd[at], self.when_even[at])

    y_low, y_high = Sorted(odd_y, y_near, y_far), Sorted(odd_y, y_far, y_near)
    y_own_low, y_own_high = Sorted(odd_y, y_own_near, y_own_far), Sorted(odd_y, y_own_far, y_own_near)
    x_low, x_high = Sorted(odd_x, x_near, x_far), Sorted(odd_x, x_far, x_near)
    x_own_low, x_own_high = Sorted(odd_x, x_own_near, x_own_far), Sorted(odd_x, x_own_far, x_own_near)
    grab = lambda ref: [ref[c] for c in range(5)]
    add = coupled(jac, 0, 1.0, x_own_low[10], x_own_low[11], grab(x_low))
    for c in range(5):
        field[c, 1] = field[c, 1] + add[c]
    add = coupled(jac, 0, -1.0, x_own_high[10], x_own_high[11], grab(x_high))
    for c in range(5):
        field[c, size_x] = field[c, size_x] + add[c]
    add_low = coupled(jac, 1, 1.0, y_own_low[10], y_own_low[11], grab(y_low))
    add_high = coupled(jac, 1, -1.0, y_own_high[10], y_own_high[11], grab(y_high))
    for c in range(5):
        for x in range(size_x):
            field[c, 1 + x, 0:1, :] = field[c, 1 + x, 0:1, :] + add_low[c][x:x + 1]
            field[c, 1 + x, size_y - 1:size_y, :] = field[c, 1 + x, size_y - 1:size_y, :] + add_high[c][x:x + 1]
    add = coupled(jac, 0, -1.0, x_low[10], x_low[11], grab(x_own_low))
    for c in range(5):
        field[c, 0] = x_low[5 + c] + add[c]
    add = coupled(jac, 0, 1.0, x_high[10], x_high[11], grab(x_own_high))
    for c in range(5):
        field[c, size_x + 1] = x_high[5 + c] + add[c]
    at_x = lax.broadcasted_iota(jnp.int32, (size_x, size_z), 0)
    for edge, theirs, own, side, corner in ((edge_low, y_low, y_own_low, -1.0, 0), (edge_high, y_high, y_own_high, 1.0, 5)):
        add = coupled(jac, 1, side, theirs[10], theirs[11], grab(own))
        speed = theirs[12]
        damping = theirs[11]
        first = [x_low[12, corner + c:corner + c + 1, :] for c in range(5)]
        last = [x_high[12, corner + c:corner + c + 1, :] for c in range(5)]
        add_first = coupled(jac, 0, 1.0, speed[0:1], damping[0:1], first)
        add_last = coupled(jac, 0, -1.0, speed[size_x - 1:size_x], damping[size_x - 1:size_x], last)
        for c in range(5):
            value = theirs[5 + c] + add[c]
            value = value + jnp.where(at_x == 0, add_first[c], 0.0)
            edge[c] = value + jnp.where(at_x == size_x - 1, add_last[c], 0.0)

    def step(x, carry):
        here = [field[c, x + 1] for c in range(5)]
        below = [field[c, x] for c in range(5)]
        above = [field[c, x + 2] for c in range(5)]
        lows = [edge_low[c, pl.ds(x, 1), :] for c in range(5)]
        highs = [edge_high[c, pl.ds(x, 1), :] for c in range(5)]
        src = [source[c, x] for c in range(5)]
        speed = [velocity[d, x].astype(jnp.float32) for d in range(3)]
        damping = dissip[x].astype(jnp.float32)
        sym = [walls[m, x] for m in range(6)]
        wall = [[sym[SYM[a][b]] for b in range(3)] for a in range(3)]
        out = relax_row(jac, here, below, above, lows, highs, src, speed, damping, wall)
        for c in range(5):
            relaxed[c, x] = out[c]
        return carry

    lax.fori_loop(0, size_x, step, 0, unroll=2)
    done = pltpu.make_async_copy(relaxed, relaxed_hbm, out_sem)
    done.start()

    normal = [plan[c:c + 1] for c in range(3)]
    strength, rank, label = plan[3:4], plan[4:5], plan[5:6]
    cell_row, depth, at_z, target_row = [plan[i:i + 1].astype(jnp.int32) for i in range(6, 10)]
    rows = one_hot(cell_row, size_x * size_y)
    turned = []
    for c in range(3):
        high, low = halves(relaxed[1 + c].reshape(size_x * size_y, size_z).T)
        turned.append(jnp.concatenate([high, low], axis=1))
    picked = jnp.dot(jnp.concatenate(turned, axis=0), jnp.concatenate([rows, rows], axis=0),
                     preferred_element_type=jnp.float32)
    along = normal[0] * picked[:size_z] + normal[1] * picked[size_z:2 * size_z] + normal[2] * picked[2 * size_z:]
    at = lax.broadcasted_iota(jnp.int32, (size_z, faces), 0) == depth
    project = jnp.sum(jnp.where(at, along, 0.0), axis=0, keepdims=True)
    scale = strength * project
    n_y, n_z, n_c, n_x = parts
    words = [normal[0] * scale, normal[1] * scale, normal[2] * scale, label]
    pair = [jnp.where(rank == float(j), w, 0.0) for j in range(2) for w in words]
    high, low = halves(jnp.concatenate(pair * n_z, axis=0))
    lane = lax.broadcasted_iota(jnp.int32, (8 * n_z, faces), 0)
    hot = jnp.where(lane // 8 == at_z, 1.0, 0.0).astype(jnp.bfloat16)
    target = one_hot(target_row, n_y * n_c * n_x)
    message[...] = dot_last(jnp.concatenate([target, target], axis=1),
                            jnp.concatenate([hot * high, hot * low], axis=1))
    done.wait()


def turn_kernel(got, out):
    turned = got[...].T
    blank = jnp.zeros((turned.shape[0], out.shape[1] - turned.shape[1]), jnp.float32)
    out[...] = jnp.concatenate([turned, blank], axis=1)


def last_kernel(used, got, out):
    tris = out.shape[1]
    rows = got.shape[0]
    fold = max(1, min(128 // used, rows // 8))
    rows = rows // fold
    packed = jnp.concatenate([got[g * rows:(g + 1) * rows, 0:used] for g in range(fold)], axis=1)
    at = lax.broadcasted_iota(jnp.int32, (tris, fold * used), 0).astype(jnp.float32)
    values, hot = [], []
    for r in range(0, rows, 8):
        tile = packed[r:r + 8]
        for j in range(2):
            high, low = halves(tile if j == 0 else pltpu.roll(tile, 4, 0))
            both = jnp.concatenate([high.astype(jnp.float32), low.astype(jnp.float32)], axis=0)
            values.append(both.astype(jnp.bfloat16))
            hot.append(jnp.where(at == tile[4 * j + 3:4 * j + 4], 1.0, 0.0).astype(jnp.bfloat16))
    total = dot_last(jnp.concatenate(values, axis=1), jnp.concatenate(hot, axis=1))
    out[...] = total[0:3] + total[8:11]


def swap(axis, near, far):
    count = lax.axis_size(axis)
    inside = [(i, i ^ 1) for i in range(count)]
    across = [(i, i + 1 if i % 2 else i - 1) for i in range(1, count - 1)]
    from_far = lax.ppermute(far, axis, across)
    return lax.ppermute(near, axis, inside), from_far


SFC = ("y", "z", "core")


def on_device(adjoint, source, velocity, dissip, jacobian, cut_counts, cut_cell, face_angles, face_area, face_pressure,
              tri_owner, tri_local):
    parts = tuple(lax.axis_size(a) for a in SFC + ("blk",))
    n_y, n_z, n_c, n_x = parts
    _, size_x, size_y, size_z = adjoint.shape
    faces = cut_cell.shape[0]
    per_brick = faces // cut_counts.shape[0]
    f32 = jnp.float32
    smem = pl.BlockSpec(memory_space=pltpu.SMEM)
    vmem = pl.BlockSpec(memory_space=pltpu.VMEM)
    hbm = pl.BlockSpec(memory_space=pltpu.HBM)
    shape = jax.ShapeDtypeStruct
    owner = tri_owner.reshape(faces)
    jacobian = jnp.transpose(jacobian, (1, 0, 2))

    strip = shape((13, 16, size_z), f32)
    block = shape(adjoint.shape, f32)
    wall = shape((6, size_x, size_y, size_z), f32)
    dma = pltpu.SemaphoreType.DMA
    scratch = lambda *arrays: [pltpu.VMEM(a.shape, a.dtype) for a in arrays]
    padded = shape((5, size_x + 2, size_y, size_z), f32)
    edge = shape((5, size_x, size_z), f32)
    far_memory = lambda *arrays: [pltpu.with_memory_space_constraint(a, pltpu.HBM) for a in arrays]
    far_memory = lambda *arrays: [pltpu.with_memory_space_constraint(a, pltpu.HBM) for a in arrays]
    partial, walls, y_near_out, y_far_out, near_end, far_end, face = pl.pallas_call(
        functools.partial(first_kernel, per_brick),
        in_specs=[smem, smem] + [hbm] * 7,
        out_specs=[vmem] * 7,
        out_shape=[block, wall] + [strip] * 4 + [shape((8, faces), f32)],
        scratch_shapes=scratch(cut_cell, face_angles, face_area, padded, source, velocity, dissip)
        + [pltpu.VMEM((2,) + strip.shape, f32), dma((7,))],
        compiler_params=ROOM,
        name="first_step",
    )(*far_memory(jacobian, cut_counts, cut_cell, face_angles, face_area, adjoint, source, velocity, dissip))
    from_near, from_far = swap("blk", y_near_out, y_far_out)

    def edge_rows(is_near, end):
        return pl.pallas_call(
            functools.partial(edge_kernel, is_near),
            in_specs=[smem] + [vmem] * 3,
            out_specs=vmem,
            out_shape=strip,
            compiler_params=SMALL,
            name="edge_rows",
        )(jacobian, from_near, from_far, end)

    x_far_out = edge_rows(False, far_end)
    x_near_out = edge_rows(True, near_end)
    x_near, x_far = swap(SFC, x_near_out, x_far_out)

    plan = pl.pallas_call(
        functools.partial(plan_kernel, per_brick, parts),
        in_specs=[pl.BlockSpec(memory_space=pl.ANY)] + [vmem] * 5,
        out_specs=vmem,
        out_shape=shape((16, faces), f32),
        compiler_params=SMALL,
        name="face_plan",
    )(x_near_out, face, cut_cell, face_pressure, owner, tri_local)

    relaxed, message = pl.pallas_call(
        functools.partial(third_kernel, parts),
        in_specs=[smem] + [vmem] * 14,
        out_specs=[hbm, vmem],
        out_shape=[block, shape((n_y * n_c * n_x, 8 * n_z), f32)],
        scratch_shapes=scratch(padded, edge, edge, block) + [dma],
        compiler_params=ROOM,
        name="second_step",
    )(jacobian, plan, partial, walls, source, velocity, dissip, y_near_out, y_far_out, from_near, from_far,
      x_near_out, x_far_out, x_near, x_far)

    got = lax.all_to_all(message, ("y", "core", "blk"), split_axis=0, concat_axis=0, tiled=True)
    turned = pl.pallas_call(
        turn_kernel,
        in_specs=[vmem],
        out_specs=vmem,
        out_shape=shape((8 * n_z, 128), f32),
        compiler_params=SMALL,
        name="turn_words",
    )(got)
    got = lax.all_to_all(turned, "z", split_axis=0, concat_axis=0, tiled=True)
    sensitivity = pl.pallas_call(
        functools.partial(last_kernel, n_y * n_c * n_x),
        in_specs=[vmem],
        out_specs=vmem,
        out_shape=shape((3, TRI_DEV), f32),
        compiler_params=SMALL,
        name="sum_terms",
    )(got)
    return relaxed, sensitivity


def solution(mesh):
    n_sfc, n_blk = mesh.shape["sfc"], mesh.shape["blk"]
    n_z = min(16, n_sfc // 2)
    split = jax.sharding.Mesh(mesh.devices.reshape(n_sfc // (2 * n_z), n_z, 2, n_blk), SFC + ("blk",))
    grid = P(None, SFC, "blk", None)
    both = SFC + ("blk",)
    return jax.shard_map(
        on_device,
        mesh=split,
        in_specs=(grid, grid, grid, P(SFC, "blk", None), P(), P(both), P(both), P(None, both), P(both), P(both),
                  P(both, None), P(both)),
        out_specs=(grid, P(None, both)),
        check_vma=False,
    )
```

```python
import functools

import jax
import jax.numpy as jnp
from jax import lax
from jax.experimental import pallas as pl
from jax.experimental.pallas import tpu as pltpu
from jax.sharding import PartitionSpec as P

TRI_DEV = 256
OMEGA = 0.8
ROOM = pltpu.CompilerParams(vmem_limit_bytes=20 * 1024 * 1024)

SMALL = pltpu.CompilerParams(vmem_limit_bytes=4 * 1024 * 1024)


def dot_last(a, b):
    return lax.dot_general(a, b, (((1,), (1,)), ((), ())), preferred_element_type=jnp.float32)


def halves(x):
    high = x.astype(jnp.bfloat16)
    return high, (x - high.astype(jnp.float32)).astype(jnp.bfloat16)


def relax_factor(damping):
    return OMEGA / (6.0 * damping + 1.0)


def face_normals(angles):
    cosine = jnp.cos(angles)
    sine = jnp.sin(angles)
    across = cosine[1:2]
    return cosine[0:1] * across, sine[0:1] * across, sine[1:2]


def one_hot(index, size):
    at = lax.broadcasted_iota(jnp.int32, (size, index.shape[1]), 0)
    return jnp.where(at == index, 1.0, 0.0).astype(jnp.bfloat16)


def cell_depth(cell, per_brick):
    position = lax.broadcasted_iota(jnp.int32, cell.shape, 1)
    return position // per_brick * 16 + cell % 16


def face_weight(counts, area, per_brick):
    position = lax.broadcasted_iota(jnp.int32, area.shape, 1)
    brick = position // per_brick
    limit = jnp.zeros(area.shape, jnp.int32)
    for b in range(counts.shape[0]):
        limit = jnp.where(brick == b, counts[b], limit)
    return jnp.where(position % per_brick < limit, area, 0.0)


class Splat:
    def __init__(self, ref):
        self.ref = ref

    def __getitem__(self, at):
        k, direction, c = at
        i = (k * 3 + direction) * 5 + c
        return self.ref[i:i + 1, :]


def turn(jac, direction, values):
    out = []
    for c in range(5):
        total = jac[0, direction, c] * values[0]
        for k in range(1, 5):
            total = total + jac[k, direction, c] * values[k]
        out.append(total)
    return out


def coupled(jac, direction, side, speed, damping, values):
    factor = relax_factor(damping)
    scaled = (0.5 * side) * factor * speed
    spread = factor * damping
    turned = turn(jac, direction, values)
    return [scaled * turned[c] + spread * values[c] for c in range(5)]


def relax_row(jac, here, lead_low, lead_high, edge_low, edge_high, source, speed, damping, wall, lead=0):
    rows, lanes = here[0].shape
    at_y = lax.broadcasted_iota(jnp.int32, (rows, lanes), 0)
    at_z = lax.broadcasted_iota(jnp.int32, (rows, lanes), 1)
    total = [None] * 5
    beside = [None] * 5
    for direction in range(3):
        jumps = []
        for c in range(5):
            if direction == lead:
                low, high = lead_low[c], lead_high[c]
            elif direction < 2:
                low = jnp.where(at_y == 0, edge_low[c], pltpu.roll(here[c], 1, 0))
                high = jnp.where(at_y == rows - 1, edge_high[c], pltpu.roll(here[c], rows - 1, 0))
            else:
                low = jnp.where(at_z == 0, 0.0, pltpu.roll(here[c], 1, 1))
                high = jnp.where(at_z == lanes - 1, 0.0, pltpu.roll(here[c], lanes - 1, 1))
            both = low + high
            beside[c] = both if beside[c] is None else beside[c] + both
            jumps.append(high - low)
        turned = turn(jac, direction, jumps)
        half = 0.5 * speed[direction]
        for c in range(5):
            part = half * turned[c]
            total[c] = part if total[c] is None else total[c] + part
    factor = relax_factor(damping)
    out = []
    for c in range(5):
        applied = total[c] + damping * (6.0 * here[c] - beside[c])
        if 1 <= c <= 3:
            for d in range(3):
                applied = applied + wall[c - 1][d] * here[1 + d]
        out.append(here[c] + factor * (source[c] - applied))
    return out


SYM = ((0, 1, 2), (1, 3, 4), (2, 4, 5))


def start_all(pairs, sems):
    copies = [pltpu.make_async_copy(src, dst, sems.at[i]) for i, (src, dst) in enumerate(pairs)]
    for copy in copies:
        copy.start()
    return copies


def wait_all(copies):
    for copy in copies:
        copy.wait()


def first_kernel(per_brick, jac_hbm, counts_hbm, cell_hbm, angle_hbm, area_hbm, adjoint_hbm, source_hbm, velocity_hbm, dissip_hbm,
                 walls, near_out, far_out, face_out, jac_out, jac, counts, cell_ref, angle_ref, area_ref, field, source, velocity, dissip,
                 coefficient, sems):
    size_x, size_y, size_z = dissip.shape
    copies = start_all([(cell_hbm, cell_ref), (angle_hbm, angle_ref), (area_hbm, area_ref),
                        (adjoint_hbm, field), (velocity_hbm, velocity),
                        (dissip_hbm, dissip), (source_hbm, source), (counts_hbm, counts), (jac_hbm, jac)], sems)
    odd = lax.axis_index("blk") % 2 == 1
    faces = cell_ref.shape[0]
    wait_all(copies[:3] + copies[7:8])
    cell = cell_ref[...].reshape(1, faces)
    area = area_ref[...].reshape(1, faces)
    normal = face_normals(angle_ref[...])
    weight = face_weight(counts, area, per_brick)
    rows = one_hot(cell // 16, size_x * size_y)
    depth = cell_depth(cell, per_brick)
    at = lax.broadcasted_iota(jnp.int32, (size_z, faces), 0) == depth
    hot = jnp.where(at, 1.0, 0.0).astype(jnp.bfloat16)
    face_out[...] = jnp.concatenate([*normal, weight, jnp.zeros((4, faces), jnp.float32)], axis=0)
    rows = jnp.concatenate([rows, rows], axis=1)
    pairs = ((0, 0), (0, 1), (0, 2), (1, 1), (1, 2), (2, 2))
    for m in range(0, 6, 2):
        put = []
        for a, b in pairs[m:m + 2]:
            high, low = halves(weight * normal[a] * normal[b])
            put.append(jnp.concatenate([hot * high, hot * low], axis=1))
        total = dot_last(rows, jnp.concatenate(put, axis=0))
        walls[m] = total[:, :size_z].reshape(size_x, size_y, size_z)
        walls[m + 1] = total[:, size_z:].reshape(size_x, size_y, size_z)
    wait_all(copies[3:7] + copies[8:])
    for i in range(75):
        jac_out[i:i + 1, :] = jnp.full((1, size_z), jac[i // 15, i // 5 % 3, i % 5], jnp.float32)

    for d in range(3):
        coefficient[d] = velocity[d].astype(jnp.float32)
    coefficient[3] = dissip[...].astype(jnp.float32)
    blank = jnp.zeros((size_x, size_z), jnp.float32)
    column = lambda ref, count, y: [ref[c, :, y, :] for c in range(count)]
    strips = []
    for y in (0, size_y - 1):
        here = column(field, 5, y)
        inner = column(field, 5, 1 if y == 0 else size_y - 2)
        below, above = ([blank] * 5, inner) if y == 0 else (inner, [blank] * 5)
        *speed, damping = column(coefficient, 4, y)
        sym = column(walls, 6, y)
        wall = [[sym[SYM[a][b]] for b in range(3)] for a in range(3)]
        zeros = [0.0] * 5
        out = relax_row(jac, here, below, above, zeros, zeros, column(source, 5, y), speed, damping, wall, lead=1)
        strips.append(here + out + [speed[1], damping, speed[0]])
    for f, (low, high) in enumerate(zip(*strips)):
        near_out[f] = jnp.where(odd, low, high)
        far_out[f] = jnp.where(odd, high, low)


def inner_kernel(jac_ref, adjoint, source, velocity, dissip, walls, partial, near_end, far_end):
    size_x, size_y, size_z = dissip.shape
    jac = Splat(jac_ref)

    def step(x, carry):
        here = [adjoint[c, x] for c in range(5)]
        has_low, has_high = jnp.where(x > 0, 1.0, 0.0), jnp.where(x < size_x - 1, 1.0, 0.0)
        below = [adjoint[c, jnp.maximum(x - 1, 0)] * has_low for c in range(5)]
        above = [adjoint[c, jnp.minimum(x + 1, size_x - 1)] * has_high for c in range(5)]
        zeros = [0.0] * 5
        src = [source[c, x] for c in range(5)]
        speed = [velocity[d, x].astype(jnp.float32) for d in range(3)]
        damping = dissip[x].astype(jnp.float32)
        sym = [walls[m, x] for m in range(6)]
        wall = [[sym[SYM[a][b]] for b in range(3)] for a in range(3)]
        out = relax_row(jac, here, below, above, zeros, zeros, src, speed, damping, wall)
        for c in range(5):
            partial[c, x] = out[c]
        return carry

    lax.fori_loop(0, size_x, step, 0, unroll=2)
    odd = lax.axis_index("core")
    for out, x in ((near_end, (1 - odd) * (size_x - 1)), (far_end, odd * (size_x - 1))):
        for c in range(5):
            out[c] = adjoint[c, x]
            out[5 + c] = partial[c, x]
        out[10] = velocity[0, x].astype(jnp.float32)
        out[11] = dissip[x].astype(jnp.float32)
        out[12] = velocity[1, x].astype(jnp.float32)


def edge_kernel(is_near, jac_ref, from_near, from_far, mine, out):
    rows, lanes = mine.shape[1:]
    jac = Splat(jac_ref)
    at_y = lax.broadcasted_iota(jnp.int32, (rows, lanes), 0)
    odd_y = lax.axis_index("blk") % 2 == 1
    last = (lax.axis_index("core") == 1) != is_near
    end = from_near.shape[1] - 1
    near = [jnp.where(last, from_near[c, end:end + 1, :], from_near[c, 0:1, :]) for c in range(5)]
    far = [jnp.where(last, from_far[c, end:end + 1, :], from_far[c, 0:1, :]) for c in range(5)]
    low = [jnp.where(odd_y, a, b) for a, b in zip(near, far)]
    high = [jnp.where(odd_y, b, a) for a, b in zip(near, far)]
    speed_y = mine[12]
    damping = mine[11]
    add_low = coupled(jac, 1, 1.0, speed_y[0:1], damping[0:1], low)
    add_high = coupled(jac, 1, -1.0, speed_y[rows - 1:rows], damping[rows - 1:rows], high)
    for c in range(5):
        out[c] = mine[c]
        fixed = mine[5 + c]
        fixed = fixed + jnp.where(at_y == 0, add_low[c], 0.0)
        out[5 + c] = fixed + jnp.where(at_y == rows - 1, add_high[c], 0.0)
    out[10] = mine[10]
    out[11] = damping
    out[12] = jnp.concatenate(low + high + [jnp.zeros((rows - 10, lanes), jnp.float32)], axis=0)


def plan_kernel(per_brick, parts, after, face, cell_ref, pressure_ref, owner_ref, local_ref, plan):
    del after
    faces = cell_ref.shape[0]
    cell = cell_ref[...].reshape(1, faces)
    owner = owner_ref[...].reshape(1, faces)
    strength = pressure_ref[...].reshape(1, faces) * face[3:4]
    label = local_ref[...].reshape(1, faces).astype(jnp.float32)
    block = min(faces, 128)
    number = owner.astype(jnp.float32)
    columns = [jnp.broadcast_to(number[:, t:t + block], (block, block)).T for t in range(0, faces, block)]
    before = (lax.broadcasted_iota(jnp.int32, (block, block), 0)
              < lax.broadcasted_iota(jnp.int32, (block, block), 1))
    ranks = []
    for u in range(faces // block):
        mine = number[:, u * block:(u + 1) * block]
        same = jnp.where((columns[u] == mine) & before, 1.0, 0.0)
        for t in range(u):
            same = same + jnp.where(columns[t] == mine, 1.0, 0.0)
        ranks.append(jnp.sum(same, axis=0, keepdims=True))
    rank = jnp.concatenate(ranks, axis=1)
    n_y, n_z, n_c, n_x = parts
    at_x, at_c, at_z, at_y = owner % n_x, owner // n_x % n_c, owner // (n_x * n_c) % n_z, owner // (n_x * n_c * n_z)
    whole = [cell // 16, cell_depth(cell, per_brick), at_z, (at_y * n_c + at_c) * n_x + at_x]
    rows = [face[0:1], face[1:2], face[2:3], strength, rank, label] + [w.astype(jnp.float32) for w in whole]
    plan[...] = jnp.concatenate(rows + [jnp.zeros((16 - len(rows), faces), jnp.float32)], axis=0)


def third_kernel(parts, jac_ref, plan, partial, walls, source, velocity, dissip, y_own_near, y_own_far, y_near, y_far,
                 x_own_near, x_own_far, x_near, x_far, relaxed_hbm, message,
                 field, edge_low, edge_high, relaxed, out_sem):
    jac = Splat(jac_ref)
    faces = plan.shape[1]
    size_x, size_y, size_z = dissip.shape
    for c in range(5):
        field[c, 1:1 + size_x] = partial[c]
    odd_y = lax.axis_index("blk") % 2 == 1
    odd_x = lax.axis_index("core") == 1

    class Sorted:
        def __init__(self, odd, when_odd, when_even):
            self.odd, self.when_odd, self.when_even = odd, when_odd, when_even

        def __getitem__(self, at):
            return jnp.where(self.odd, self.when_odd[at], self.when_even[at])

    y_low, y_high = Sorted(odd_y, y_near, y_far), Sorted(odd_y, y_far, y_near)
    y_own_low, y_own_high = Sorted(odd_y, y_own_near, y_own_far), Sorted(odd_y, y_own_far, y_own_near)
    x_low, x_high = Sorted(odd_x, x_near, x_far), Sorted(odd_x, x_far, x_near)
    x_own_low, x_own_high = Sorted(odd_x, x_own_near, x_own_far), Sorted(odd_x, x_own_far, x_own_near)
    grab = lambda ref: [ref[c] for c in range(5)]
    add = coupled(jac, 0, 1.0, x_own_low[10], x_own_low[11], grab(x_low))
    for c in range(5):
        field[c, 1] = field[c, 1] + add[c]
    add = coupled(jac, 0, -1.0, x_own_high[10], x_own_high[11], grab(x_high))
    for c in range(5):
        field[c, size_x] = field[c, size_x] + add[c]
    add_low = coupled(jac, 1, 1.0, y_own_low[10], y_own_low[11], grab(y_low))
    add_high = coupled(jac, 1, -1.0, y_own_high[10], y_own_high[11], grab(y_high))
    for c in range(5):
        for x in range(size_x):
            field[c, 1 + x, 0:1, :] = field[c, 1 + x, 0:1, :] + add_low[c][x:x + 1]
            field[c, 1 + x, size_y - 1:size_y, :] = field[c, 1 + x, size_y - 1:size_y, :] + add_high[c][x:x + 1]
    add = coupled(jac, 0, -1.0, x_low[10], x_low[11], grab(x_own_low))
    for c in range(5):
        field[c, 0] = x_low[5 + c] + add[c]
    add = coupled(jac, 0, 1.0, x_high[10], x_high[11], grab(x_own_high))
    for c in range(5):
        field[c, size_x + 1] = x_high[5 + c] + add[c]
    at_x = lax.broadcasted_iota(jnp.int32, (size_x, size_z), 0)
    for edge, theirs, own, side, corner in ((edge_low, y_low, y_own_low, -1.0, 0), (edge_high, y_high, y_own_high, 1.0, 5)):
        add = coupled(jac, 1, side, theirs[10], theirs[11], grab(own))
        speed = theirs[12]
        damping = theirs[11]
        first = [x_low[12, corner + c:corner + c + 1, :] for c in range(5)]
        last = [x_high[12, corner + c:corner + c + 1, :] for c in range(5)]
        add_first = coupled(jac, 0, 1.0, speed[0:1], damping[0:1], first)
        add_last = coupled(jac, 0, -1.0, speed[size_x - 1:size_x], damping[size_x - 1:size_x], last)
        for c in range(5):
            value = theirs[5 + c] + add[c]
            value = value + jnp.where(at_x == 0, add_first[c], 0.0)
            edge[c] = value + jnp.where(at_x == size_x - 1, add_last[c], 0.0)

    def step(x, carry):
        here = [field[c, x + 1] for c in range(5)]
        below = [field[c, x] for c in range(5)]
        above = [field[c, x + 2] for c in range(5)]
        lows = [edge_low[c, pl.ds(x, 1), :] for c in range(5)]
        highs = [edge_high[c, pl.ds(x, 1), :] for c in range(5)]
        src = [source[c, x] for c in range(5)]
        speed = [velocity[d, x].astype(jnp.float32) for d in range(3)]
        damping = dissip[x].astype(jnp.float32)
        sym = [walls[m, x] for m in range(6)]
        wall = [[sym[SYM[a][b]] for b in range(3)] for a in range(3)]
        out = relax_row(jac, here, below, above, lows, highs, src, speed, damping, wall)
        for c in range(5):
            relaxed[c, x] = out[c]
        return carry

    lax.fori_loop(0, size_x, step, 0, unroll=2)
    done = pltpu.make_async_copy(relaxed, relaxed_hbm, out_sem)
    done.start()

    normal = [plan[c:c + 1] for c in range(3)]
    strength, rank, label = plan[3:4], plan[4:5], plan[5:6]
    cell_row, depth, at_z, target_row = [plan[i:i + 1].astype(jnp.int32) for i in range(6, 10)]
    rows = one_hot(cell_row, size_x * size_y)
    turned = []
    for c in range(3):
        high, low = halves(relaxed[1 + c].reshape(size_x * size_y, size_z).T)
        turned.append(jnp.concatenate([high, low], axis=1))
    picked = jnp.dot(jnp.concatenate(turned, axis=0), jnp.concatenate([rows, rows], axis=0),
                     preferred_element_type=jnp.float32)
    along = normal[0] * picked[:size_z] + normal[1] * picked[size_z:2 * size_z] + normal[2] * picked[2 * size_z:]
    at = lax.broadcasted_iota(jnp.int32, (size_z, faces), 0) == depth
    project = jnp.sum(jnp.where(at, along, 0.0), axis=0, keepdims=True)
    scale = strength * project
    n_y, n_z, n_c, n_x = parts
    words = [normal[0] * scale, normal[1] * scale, normal[2] * scale, label]
    pair = [jnp.where(rank == float(j), w, 0.0) for j in range(2) for w in words]
    high, low = halves(jnp.concatenate(pair * n_z, axis=0))
    lane = lax.broadcasted_iota(jnp.int32, (8 * n_z, faces), 0)
    hot = jnp.where(lane // 8 == at_z, 1.0, 0.0).astype(jnp.bfloat16)
    target = one_hot(target_row, n_y * n_c * n_x)
    message[...] = dot_last(jnp.concatenate([target, target], axis=1),
                            jnp.concatenate([hot * high, hot * low], axis=1))
    done.wait()


def turn_kernel(got, out):
    turned = got[...].T
    blank = jnp.zeros((turned.shape[0], out.shape[1] - turned.shape[1]), jnp.float32)
    out[...] = jnp.concatenate([turned, blank], axis=1)


def last_kernel(used, got, out):
    tris = out.shape[1]
    rows = got.shape[0]
    fold = max(1, min(128 // used, rows // 8))
    rows = rows // fold
    packed = jnp.concatenate([got[g * rows:(g + 1) * rows, 0:used] for g in range(fold)], axis=1)
    at = lax.broadcasted_iota(jnp.int32, (tris, fold * used), 0).astype(jnp.float32)
    values, hot = [], []
    for r in range(0, rows, 8):
        tile = packed[r:r + 8]
        for j in range(2):
            high, low = halves(tile if j == 0 else pltpu.roll(tile, 4, 0))
            both = jnp.concatenate([high.astype(jnp.float32), low.astype(jnp.float32)], axis=0)
            values.append(both.astype(jnp.bfloat16))
            hot.append(jnp.where(at == tile[4 * j + 3:4 * j + 4], 1.0, 0.0).astype(jnp.bfloat16))
    total = dot_last(jnp.concatenate(values, axis=1), jnp.concatenate(hot, axis=1))
    out[...] = total[0:3] + total[8:11]


def swap(axis, near, far):
    count = lax.axis_size(axis)
    inside = [(i, i ^ 1) for i in range(count)]
    across = [(i, i + 1 if i % 2 else i - 1) for i in range(1, count - 1)]
    from_far = lax.ppermute(far, axis, across)
    return lax.ppermute(near, axis, inside), from_far


SFC = ("y", "z", "core")


def on_device(adjoint, source, velocity, dissip, jacobian, cut_counts, cut_cell, face_angles, face_area, face_pressure,
              tri_owner, tri_local):
    parts = tuple(lax.axis_size(a) for a in SFC + ("blk",))
    n_y, n_z, n_c, n_x = parts
    _, size_x, size_y, size_z = adjoint.shape
    faces = cut_cell.shape[0]
    per_brick = faces // cut_counts.shape[0]
    f32 = jnp.float32
    vmem = pl.BlockSpec(memory_space=pltpu.VMEM)
    hbm = pl.BlockSpec(memory_space=pltpu.HBM)
    shape = jax.ShapeDtypeStruct
    owner = tri_owner.reshape(faces)
    jacobian = jnp.transpose(jacobian, (1, 0, 2))

    strip = shape((13, 16, size_z), f32)
    block = shape(adjoint.shape, f32)
    wall = shape((6, size_x, size_y, size_z), f32)
    dma = pltpu.SemaphoreType.DMA
    scratch = lambda *arrays: [pltpu.VMEM(a.shape, a.dtype) for a in arrays]
    padded = shape((5, size_x + 2, size_y, size_z), f32)
    edge = shape((5, size_x, size_z), f32)
    far_memory = lambda *arrays: [pltpu.with_memory_space_constraint(a, pltpu.HBM) for a in arrays]
    far_memory = lambda *arrays: [pltpu.with_memory_space_constraint(a, pltpu.HBM) for a in arrays]
    walls, y_near_out, y_far_out, face, jac_rows = pl.pallas_call(
        functools.partial(first_kernel, per_brick),
        in_specs=[hbm] * 9,
        out_specs=[vmem] * 5,
        out_shape=[wall, strip, strip, shape((8, faces), f32), shape((80, size_z), f32)],
        scratch_shapes=[pltpu.SMEM(jacobian.shape, f32), pltpu.SMEM(cut_counts.shape, jnp.int32)] + scratch(cut_cell, face_angles, face_area, block, source, velocity, dissip)
        + [pltpu.VMEM((4,) + dissip.shape, f32), dma((9,))],
        compiler_params=ROOM,
        name="first_columns",
    )(*far_memory(jacobian, cut_counts, cut_cell, face_angles, face_area, adjoint, source, velocity, dissip))
    from_near, from_far = swap("blk", y_near_out, y_far_out)

    partial, near_end, far_end = pl.pallas_call(
        inner_kernel,
        in_specs=[vmem] * 6,
        out_specs=[vmem] * 3,
        out_shape=[block, strip, strip],
        compiler_params=ROOM,
        name="first_step",
    )(jac_rows, adjoint, source, velocity, dissip, walls)

    def edge_rows(is_near, end):
        return pl.pallas_call(
            functools.partial(edge_kernel, is_near),
            in_specs=[vmem] * 4,
            out_specs=vmem,
            out_shape=strip,
            compiler_params=SMALL,
            name="edge_rows",
        )(jac_rows, from_near, from_far, end)

    x_far_out = edge_rows(False, far_end)
    x_near_out = edge_rows(True, near_end)
    x_near, x_far = swap(SFC, x_near_out, x_far_out)

    plan = pl.pallas_call(
        functools.partial(plan_kernel, per_brick, parts),
        in_specs=[pl.BlockSpec(memory_space=pl.ANY)] + [vmem] * 5,
        out_specs=vmem,
        out_shape=shape((16, faces), f32),
        compiler_params=SMALL,
        name="face_plan",
    )(x_near_out, face, cut_cell, face_pressure, owner, tri_local)

    relaxed, message = pl.pallas_call(
        functools.partial(third_kernel, parts),
        in_specs=[vmem] * 15,
        out_specs=[hbm, vmem],
        out_shape=[block, shape((n_y * n_c * n_x, 8 * n_z), f32)],
        scratch_shapes=scratch(padded, edge, edge, block) + [dma],
        compiler_params=ROOM,
        name="second_step",
    )(jac_rows, plan, partial, walls, source, velocity, dissip, y_near_out, y_far_out, from_near, from_far,
      x_near_out, x_far_out, x_near, x_far)

    got = lax.all_to_all(message, ("y", "core", "blk"), split_axis=0, concat_axis=0, tiled=True)
    turned = pl.pallas_call(
        turn_kernel,
        in_specs=[vmem],
        out_specs=vmem,
        out_shape=shape((8 * n_z, 128), f32),
        compiler_params=SMALL,
        name="turn_words",
    )(got)
    got = lax.all_to_all(turned, "z", split_axis=0, concat_axis=0, tiled=True)
    sensitivity = pl.pallas_call(
        functools.partial(last_kernel, n_y * n_c * n_x),
        in_specs=[vmem],
        out_specs=vmem,
        out_shape=shape((3, TRI_DEV), f32),
        compiler_params=SMALL,
        name="sum_terms",
    )(got)
    return relaxed, sensitivity


def solution(mesh):
    n_sfc, n_blk = mesh.shape["sfc"], mesh.shape["blk"]
    n_z = min(16, n_sfc // 2)
    split = jax.sharding.Mesh(mesh.devices.reshape(n_sfc // (2 * n_z), n_z, 2, n_blk), SFC + ("blk",))
    grid = P(None, SFC, "blk", None)
    both = SFC + ("blk",)
    return jax.shard_map(
        on_device,
        mesh=split,
        in_specs=(grid, grid, grid, P(SFC, "blk", None), P(), P(both), P(both), P(None, both), P(both), P(both),
                  P(both, None), P(both)),
        out_specs=(grid, P(None, both)),
        check_vma=False,
    )
```

```python
import functools

import jax
import jax.numpy as jnp
from jax import lax
from jax.experimental import pallas as pl
from jax.experimental.pallas import tpu as pltpu
from jax.sharding import PartitionSpec as P

TRI_DEV = 256
OMEGA = 0.8
ROOM = pltpu.CompilerParams(vmem_limit_bytes=20 * 1024 * 1024)

SMALL = pltpu.CompilerParams(vmem_limit_bytes=4 * 1024 * 1024)


def dot_last(a, b):
    return lax.dot_general(a, b, (((1,), (1,)), ((), ())), preferred_element_type=jnp.float32)


def halves(x):
    high = x.astype(jnp.bfloat16)
    return high, (x - high.astype(jnp.float32)).astype(jnp.bfloat16)


def relax_factor(damping):
    return OMEGA / (6.0 * damping + 1.0)


def face_normals(angles):
    cosine = jnp.cos(angles)
    sine = jnp.sin(angles)
    across = cosine[1:2]
    return cosine[0:1] * across, sine[0:1] * across, sine[1:2]


def one_hot(index, size):
    at = lax.broadcasted_iota(jnp.int32, (size, index.shape[1]), 0)
    return jnp.where(at == index, 1.0, 0.0).astype(jnp.bfloat16)


def cell_depth(cell, per_brick):
    position = lax.broadcasted_iota(jnp.int32, cell.shape, 1)
    return position // per_brick * 16 + cell % 16


def face_weight(counts, area, per_brick):
    position = lax.broadcasted_iota(jnp.int32, area.shape, 1)
    brick = position // per_brick
    limit = jnp.zeros(area.shape, jnp.int32)
    for b in range(counts.shape[0]):
        limit = jnp.where(brick == b, counts[b], limit)
    return jnp.where(position % per_brick < limit, area, 0.0)


class Splat:
    def __init__(self, ref):
        self.ref = ref

    def __getitem__(self, at):
        k, direction, c = at
        i = (k * 3 + direction) * 5 + c
        return self.ref[i:i + 1, :]


def turn(jac, direction, values):
    out = []
    for c in range(5):
        total = jac[0, direction, c] * values[0]
        for k in range(1, 5):
            total = total + jac[k, direction, c] * values[k]
        out.append(total)
    return out


def coupled(jac, direction, side, speed, damping, values):
    factor = relax_factor(damping)
    scaled = (0.5 * side) * factor * speed
    spread = factor * damping
    turned = turn(jac, direction, values)
    return [scaled * turned[c] + spread * values[c] for c in range(5)]


def relax_row(jac, here, lead_low, lead_high, edge_low, edge_high, source, speed, damping, wall, lead=0):
    rows, lanes = here[0].shape
    at_y = lax.broadcasted_iota(jnp.int32, (rows, lanes), 0)
    at_z = lax.broadcasted_iota(jnp.int32, (rows, lanes), 1)
    total = [None] * 5
    beside = [None] * 5
    for direction in range(3):
        jumps = []
        for c in range(5):
            if direction == lead:
                low, high = lead_low[c], lead_high[c]
            elif direction < 2:
                low = jnp.where(at_y == 0, edge_low[c], pltpu.roll(here[c], 1, 0))
                high = jnp.where(at_y == rows - 1, edge_high[c], pltpu.roll(here[c], rows - 1, 0))
            else:
                low = jnp.where(at_z == 0, 0.0, pltpu.roll(here[c], 1, 1))
                high = jnp.where(at_z == lanes - 1, 0.0, pltpu.roll(here[c], lanes - 1, 1))
            both = low + high
            beside[c] = both if beside[c] is None else beside[c] + both
            jumps.append(high - low)
        turned = turn(jac, direction, jumps)
        half = 0.5 * speed[direction]
        for c in range(5):
            part = half * turned[c]
            total[c] = part if total[c] is None else total[c] + part
    factor = relax_factor(damping)
    out = []
    for c in range(5):
        applied = total[c] + damping * (6.0 * here[c] - beside[c])
        if 1 <= c <= 3:
            for d in range(3):
                applied = applied + wall[c - 1][d] * here[1 + d]
        out.append(here[c] + factor * (source[c] - applied))
    return out


SYM = ((0, 1, 2), (1, 3, 4), (2, 4, 5))


def start_all(pairs, sems):
    copies = [pltpu.make_async_copy(src, dst, sems.at[i]) for i, (src, dst) in enumerate(pairs)]
    for copy in copies:
        copy.start()
    return copies


def wait_all(copies):
    for copy in copies:
        copy.wait()


def first_kernel(per_brick, jac_hbm, counts_hbm, cell_hbm, angle_hbm, area_hbm, adjoint_hbm, source_hbm, velocity_hbm, dissip_hbm,
                 walls, near_out, far_out, face_out, jac_out, jac, counts, cell_ref, angle_ref, area_ref, field, source, velocity, dissip,
                 coefficient, sems):
    size_x, size_y, size_z = dissip.shape
    copies = start_all([(cell_hbm, cell_ref), (angle_hbm, angle_ref), (area_hbm, area_ref),
                        (adjoint_hbm, field), (velocity_hbm, velocity),
                        (dissip_hbm, dissip), (source_hbm, source), (counts_hbm, counts), (jac_hbm, jac)], sems)
    odd = lax.axis_index("blk") % 2 == 1
    faces = cell_ref.shape[0]
    wait_all(copies[:3] + copies[7:8])
    cell = cell_ref[...].reshape(1, faces)
    area = area_ref[...].reshape(1, faces)
    normal = face_normals(angle_ref[...])
    weight = face_weight(counts, area, per_brick)
    rows = one_hot(cell // 16, size_x * size_y)
    depth = cell_depth(cell, per_brick)
    at = lax.broadcasted_iota(jnp.int32, (size_z, faces), 0) == depth
    hot = jnp.where(at, 1.0, 0.0).astype(jnp.bfloat16)
    face_out[...] = jnp.concatenate([*normal, weight, jnp.zeros((4, faces), jnp.float32)], axis=0)
    rows = jnp.concatenate([rows, rows], axis=1)
    pairs = ((0, 0), (0, 1), (0, 2), (1, 1), (1, 2), (2, 2))
    for m in range(0, 6, 2):
        put = []
        for a, b in pairs[m:m + 2]:
            high, low = halves(weight * normal[a] * normal[b])
            put.append(jnp.concatenate([hot * high, hot * low], axis=1))
        total = dot_last(rows, jnp.concatenate(put, axis=0))
        walls[m] = total[:, :size_z].reshape(size_x, size_y, size_z)
        walls[m + 1] = total[:, size_z:].reshape(size_x, size_y, size_z)
    wait_all(copies[3:7] + copies[8:])
    for i in range(75):
        jac_out[i:i + 1, :] = jnp.full((1, size_z), jac[i // 15, i // 5 % 3, i % 5], jnp.float32)

    for d in range(3):
        coefficient[d] = velocity[d].astype(jnp.float32)
    coefficient[3] = dissip[...].astype(jnp.float32)
    blank = jnp.zeros((size_x, size_z), jnp.float32)
    column = lambda ref, count, y: [ref[c, :, y, :] for c in range(count)]
    strips = []
    for y in (0, size_y - 1):
        here = column(field, 5, y)
        inner = column(field, 5, 1 if y == 0 else size_y - 2)
        below, above = ([blank] * 5, inner) if y == 0 else (inner, [blank] * 5)
        *speed, damping = column(coefficient, 4, y)
        sym = column(walls, 6, y)
        wall = [[sym[SYM[a][b]] for b in range(3)] for a in range(3)]
        zeros = [0.0] * 5
        out = relax_row(jac, here, below, above, zeros, zeros, column(source, 5, y), speed, damping, wall, lead=1)
        strips.append(here + out + [speed[1], damping, speed[0]])
    for f, (low, high) in enumerate(zip(*strips)):
        near_out[f] = jnp.where(odd, low, high)
        far_out[f] = jnp.where(odd, high, low)


def inner_kernel(jac_ref, adjoint, source, velocity, dissip, walls, partial, near_end, far_end):
    size_x, size_y, size_z = dissip.shape
    jac = Splat(jac_ref)

    def step(x, carry):
        here = [adjoint[c, x] for c in range(5)]
        has_low, has_high = jnp.where(x > 0, 1.0, 0.0), jnp.where(x < size_x - 1, 1.0, 0.0)
        below = [adjoint[c, jnp.maximum(x - 1, 0)] * has_low for c in range(5)]
        above = [adjoint[c, jnp.minimum(x + 1, size_x - 1)] * has_high for c in range(5)]
        zeros = [0.0] * 5
        src = [source[c, x] for c in range(5)]
        speed = [velocity[d, x].astype(jnp.float32) for d in range(3)]
        damping = dissip[x].astype(jnp.float32)
        sym = [walls[m, x] for m in range(6)]
        wall = [[sym[SYM[a][b]] for b in range(3)] for a in range(3)]
        out = relax_row(jac, here, below, above, zeros, zeros, src, speed, damping, wall)
        for c in range(5):
            partial[c, x] = out[c]
        return carry

    lax.fori_loop(0, size_x, step, 0, unroll=2)
    odd = lax.axis_index("core")
    for out, x in ((near_end, (1 - odd) * (size_x - 1)), (far_end, odd * (size_x - 1))):
        for c in range(5):
            out[c] = adjoint[c, x]
            out[5 + c] = partial[c, x]
        out[10] = velocity[0, x].astype(jnp.float32)
        out[11] = dissip[x].astype(jnp.float32)
        out[12] = velocity[1, x].astype(jnp.float32)


def edge_kernel(is_near, jac_ref, from_near, from_far, mine, out):
    rows, lanes = mine.shape[1:]
    jac = Splat(jac_ref)
    at_y = lax.broadcasted_iota(jnp.int32, (rows, lanes), 0)
    odd_y = lax.axis_index("blk") % 2 == 1
    last = (lax.axis_index("core") == 1) != is_near
    end = from_near.shape[1] - 1
    near = [jnp.where(last, from_near[c, end:end + 1, :], from_near[c, 0:1, :]) for c in range(5)]
    far = [jnp.where(last, from_far[c, end:end + 1, :], from_far[c, 0:1, :]) for c in range(5)]
    low = [jnp.where(odd_y, a, b) for a, b in zip(near, far)]
    high = [jnp.where(odd_y, b, a) for a, b in zip(near, far)]
    speed_y = mine[12]
    damping = mine[11]
    add_low = coupled(jac, 1, 1.0, speed_y[0:1], damping[0:1], low)
    add_high = coupled(jac, 1, -1.0, speed_y[rows - 1:rows], damping[rows - 1:rows], high)
    for c in range(5):
        out[c] = mine[c]
        fixed = mine[5 + c]
        fixed = fixed + jnp.where(at_y == 0, add_low[c], 0.0)
        out[5 + c] = fixed + jnp.where(at_y == rows - 1, add_high[c], 0.0)
    out[10] = mine[10]
    out[11] = damping
    out[12] = jnp.concatenate(low + high + [jnp.zeros((rows - 10, lanes), jnp.float32)], axis=0)


def plan_kernel(per_brick, parts, after, face, cell_ref, pressure_ref, owner_ref, local_ref, plan):
    del after
    faces = cell_ref.shape[0]
    cell = cell_ref[...].reshape(1, faces)
    owner = owner_ref[...].reshape(1, faces)
    strength = pressure_ref[...].reshape(1, faces) * face[3:4]
    label = local_ref[...].reshape(1, faces).astype(jnp.float32)
    block = min(faces, 128)
    number = owner.astype(jnp.float32)
    columns = [jnp.broadcast_to(number[:, t:t + block], (block, block)).T for t in range(0, faces, block)]
    before = (lax.broadcasted_iota(jnp.int32, (block, block), 0)
              < lax.broadcasted_iota(jnp.int32, (block, block), 1))
    ranks = []
    for u in range(faces // block):
        mine = number[:, u * block:(u + 1) * block]
        same = jnp.where((columns[u] == mine) & before, 1.0, 0.0)
        for t in range(u):
            same = same + jnp.where(columns[t] == mine, 1.0, 0.0)
        ranks.append(jnp.sum(same, axis=0, keepdims=True))
    rank = jnp.concatenate(ranks, axis=1)
    n_y, n_z, n_c, n_x = parts
    at_x, at_c, at_z, at_y = owner % n_x, owner // n_x % n_c, owner // (n_x * n_c) % n_z, owner // (n_x * n_c * n_z)
    whole = [cell // 16, cell_depth(cell, per_brick), at_z, (at_y * n_c + at_c) * n_x + at_x]
    rows = [face[0:1], face[1:2], face[2:3], strength, rank, label] + [w.astype(jnp.float32) for w in whole]
    plan[...] = jnp.concatenate(rows + [jnp.zeros((16 - len(rows), faces), jnp.float32)], axis=0)


def third_kernel(parts, jac_ref, plan, partial, walls, source, velocity, dissip, y_own_near, y_own_far, y_near, y_far,
                 x_own_near, x_own_far, x_near, x_far, relaxed_hbm, message,
                 field, edge_low, edge_high, relaxed, out_sem):
    jac = Splat(jac_ref)
    faces = plan.shape[1]
    size_x, size_y, size_z = dissip.shape
    for c in range(5):
        field[c, 1:1 + size_x] = partial[c]
    odd_y = lax.axis_index("blk") % 2 == 1
    odd_x = lax.axis_index("core") == 1

    class Sorted:
        def __init__(self, odd, when_odd, when_even):
            self.odd, self.when_odd, self.when_even = odd, when_odd, when_even

        def __getitem__(self, at):
            return jnp.where(self.odd, self.when_odd[at], self.when_even[at])

    y_low, y_high = Sorted(odd_y, y_near, y_far), Sorted(odd_y, y_far, y_near)
    y_own_low, y_own_high = Sorted(odd_y, y_own_near, y_own_far), Sorted(odd_y, y_own_far, y_own_near)
    x_low, x_high = Sorted(odd_x, x_near, x_far), Sorted(odd_x, x_far, x_near)
    x_own_low, x_own_high = Sorted(odd_x, x_own_near, x_own_far), Sorted(odd_x, x_own_far, x_own_near)
    grab = lambda ref: [ref[c] for c in range(5)]
    add = coupled(jac, 0, 1.0, x_own_low[10], x_own_low[11], grab(x_low))
    for c in range(5):
        field[c, 1] = field[c, 1] + add[c]
    add = coupled(jac, 0, -1.0, x_own_high[10], x_own_high[11], grab(x_high))
    for c in range(5):
        field[c, size_x] = field[c, size_x] + add[c]
    add_low = coupled(jac, 1, 1.0, y_own_low[10], y_own_low[11], grab(y_low))
    add_high = coupled(jac, 1, -1.0, y_own_high[10], y_own_high[11], grab(y_high))
    for c in range(5):
        for x in range(size_x):
            field[c, 1 + x, 0:1, :] = field[c, 1 + x, 0:1, :] + add_low[c][x:x + 1]
            field[c, 1 + x, size_y - 1:size_y, :] = field[c, 1 + x, size_y - 1:size_y, :] + add_high[c][x:x + 1]
    add = coupled(jac, 0, -1.0, x_low[10], x_low[11], grab(x_own_low))
    for c in range(5):
        field[c, 0] = x_low[5 + c] + add[c]
    add = coupled(jac, 0, 1.0, x_high[10], x_high[11], grab(x_own_high))
    for c in range(5):
        field[c, size_x + 1] = x_high[5 + c] + add[c]
    at_x = lax.broadcasted_iota(jnp.int32, (size_x, size_z), 0)
    for edge, theirs, own, side, corner in ((edge_low, y_low, y_own_low, -1.0, 0), (edge_high, y_high, y_own_high, 1.0, 5)):
        add = coupled(jac, 1, side, theirs[10], theirs[11], grab(own))
        speed = theirs[12]
        damping = theirs[11]
        first = [x_low[12, corner + c:corner + c + 1, :] for c in range(5)]
        last = [x_high[12, corner + c:corner + c + 1, :] for c in range(5)]
        add_first = coupled(jac, 0, 1.0, speed[0:1], damping[0:1], first)
        add_last = coupled(jac, 0, -1.0, speed[size_x - 1:size_x], damping[size_x - 1:size_x], last)
        for c in range(5):
            value = theirs[5 + c] + add[c]
            value = value + jnp.where(at_x == 0, add_first[c], 0.0)
            edge[c] = value + jnp.where(at_x == size_x - 1, add_last[c], 0.0)

    def step(x, carry):
        here = [field[c, x + 1] for c in range(5)]
        below = [field[c, x] for c in range(5)]
        above = [field[c, x + 2] for c in range(5)]
        lows = [edge_low[c, pl.ds(x, 1), :] for c in range(5)]
        highs = [edge_high[c, pl.ds(x, 1), :] for c in range(5)]
        src = [source[c, x] for c in range(5)]
        speed = [velocity[d, x].astype(jnp.float32) for d in range(3)]
        damping = dissip[x].astype(jnp.float32)
        sym = [walls[m, x] for m in range(6)]
        wall = [[sym[SYM[a][b]] for b in range(3)] for a in range(3)]
        out = relax_row(jac, here, below, above, lows, highs, src, speed, damping, wall)
        for c in range(5):
            relaxed[c, x] = out[c]
        return carry

    half = size_x // 2
    parts_out = [pl.ds(h * half, half) for h in range(2)]
    dones = [pltpu.make_async_copy(relaxed.at[:, at], relaxed_hbm.at[:, at], out_sem.at[h]) for h, at in enumerate(parts_out)]
    for h in range(2):
        lax.fori_loop(h * half, (h + 1) * half, step, 0, unroll=4)
        dones[h].start()

    normal = [plan[c:c + 1] for c in range(3)]
    strength, rank, label = plan[3:4], plan[4:5], plan[5:6]
    cell_row, depth, at_z, target_row = [plan[i:i + 1].astype(jnp.int32) for i in range(6, 10)]
    rows = one_hot(cell_row, size_x * size_y)
    turned = []
    for c in range(3):
        high, low = halves(relaxed[1 + c].reshape(size_x * size_y, size_z).T)
        turned.append(jnp.concatenate([high, low], axis=1))
    picked = jnp.dot(jnp.concatenate(turned, axis=0), jnp.concatenate([rows, rows], axis=0),
                     preferred_element_type=jnp.float32)
    along = normal[0] * picked[:size_z] + normal[1] * picked[size_z:2 * size_z] + normal[2] * picked[2 * size_z:]
    at = lax.broadcasted_iota(jnp.int32, (size_z, faces), 0) == depth
    project = jnp.sum(jnp.where(at, along, 0.0), axis=0, keepdims=True)
    scale = strength * project
    n_y, n_z, n_c, n_x = parts
    words = [normal[0] * scale, normal[1] * scale, normal[2] * scale, label]
    pair = [jnp.where(rank == float(j), w, 0.0) for j in range(2) for w in words]
    high, low = halves(jnp.concatenate(pair * n_z, axis=0))
    lane = lax.broadcasted_iota(jnp.int32, (8 * n_z, faces), 0)
    hot = jnp.where(lane // 8 == at_z, 1.0, 0.0).astype(jnp.bfloat16)
    target = one_hot(target_row, n_y * n_c * n_x)
    message[...] = dot_last(jnp.concatenate([target, target], axis=1),
                            jnp.concatenate([hot * high, hot * low], axis=1))
    wait_all(dones)


def turn_kernel(got, out):
    turned = got[...].T
    blank = jnp.zeros((turned.shape[0], out.shape[1] - turned.shape[1]), jnp.float32)
    out[...] = jnp.concatenate([turned, blank], axis=1)


def last_kernel(used, got, out):
    tris = out.shape[1]
    rows = got.shape[0]
    fold = max(1, min(128 // used, rows // 8))
    rows = rows // fold
    packed = jnp.concatenate([got[g * rows:(g + 1) * rows, 0:used] for g in range(fold)], axis=1)
    at = lax.broadcasted_iota(jnp.int32, (tris, fold * used), 0).astype(jnp.float32)
    values, hot = [], []
    for r in range(0, rows, 8):
        tile = packed[r:r + 8]
        for j in range(2):
            high, low = halves(tile if j == 0 else pltpu.roll(tile, 4, 0))
            both = jnp.concatenate([high.astype(jnp.float32), low.astype(jnp.float32)], axis=0)
            values.append(both.astype(jnp.bfloat16))
            hot.append(jnp.where(at == tile[4 * j + 3:4 * j + 4], 1.0, 0.0).astype(jnp.bfloat16))
    total = dot_last(jnp.concatenate(values, axis=1), jnp.concatenate(hot, axis=1))
    out[...] = total[0:3] + total[8:11]


def swap(axis, near, far):
    count = lax.axis_size(axis)
    inside = [(i, i ^ 1) for i in range(count)]
    across = [(i, i + 1 if i % 2 else i - 1) for i in range(1, count - 1)]
    from_far = lax.ppermute(far, axis, across)
    return lax.ppermute(near, axis, inside), from_far


SFC = ("y", "z", "core")


def on_device(adjoint, source, velocity, dissip, jacobian, cut_counts, cut_cell, face_angles, face_area, face_pressure,
              tri_owner, tri_local):
    parts = tuple(lax.axis_size(a) for a in SFC + ("blk",))
    n_y, n_z, n_c, n_x = parts
    _, size_x, size_y, size_z = adjoint.shape
    faces = cut_cell.shape[0]
    per_brick = faces // cut_counts.shape[0]
    f32 = jnp.float32
    vmem = pl.BlockSpec(memory_space=pltpu.VMEM)
    hbm = pl.BlockSpec(memory_space=pltpu.HBM)
    shape = jax.ShapeDtypeStruct
    owner = tri_owner.reshape(faces)
    jacobian = jnp.transpose(jacobian, (1, 0, 2))

    strip = shape((13, 16, size_z), f32)
    block = shape(adjoint.shape, f32)
    wall = shape((6, size_x, size_y, size_z), f32)
    dma = pltpu.SemaphoreType.DMA
    scratch = lambda *arrays: [pltpu.VMEM(a.shape, a.dtype) for a in arrays]
    padded = shape((5, size_x + 2, size_y, size_z), f32)
    edge = shape((5, size_x, size_z), f32)
    far_memory = lambda *arrays: [pltpu.with_memory_space_constraint(a, pltpu.HBM) for a in arrays]
    far_memory = lambda *arrays: [pltpu.with_memory_space_constraint(a, pltpu.HBM) for a in arrays]
    walls, y_near_out, y_far_out, face, jac_rows = pl.pallas_call(
        functools.partial(first_kernel, per_brick),
        in_specs=[hbm] * 9,
        out_specs=[vmem] * 5,
        out_shape=[wall, strip, strip, shape((8, faces), f32), shape((80, size_z), f32)],
        scratch_shapes=[pltpu.SMEM(jacobian.shape, f32), pltpu.SMEM(cut_counts.shape, jnp.int32)] + scratch(cut_cell, face_angles, face_area, block, source, velocity, dissip)
        + [pltpu.VMEM((4,) + dissip.shape, f32), dma((9,))],
        compiler_params=ROOM,
        name="first_columns",
    )(*far_memory(jacobian, cut_counts, cut_cell, face_angles, face_area, adjoint, source, velocity, dissip))
    from_near, from_far = swap("blk", y_near_out, y_far_out)

    partial, near_end, far_end = pl.pallas_call(
        inner_kernel,
        in_specs=[vmem] * 6,
        out_specs=[vmem] * 3,
        out_shape=[block, strip, strip],
        compiler_params=ROOM,
        name="first_step",
    )(jac_rows, adjoint, source, velocity, dissip, walls)

    def edge_rows(is_near, end):
        return pl.pallas_call(
            functools.partial(edge_kernel, is_near),
            in_specs=[vmem] * 4,
            out_specs=vmem,
            out_shape=strip,
            compiler_params=SMALL,
            name="edge_rows",
        )(jac_rows, from_near, from_far, end)

    x_far_out = edge_rows(False, far_end)
    x_near_out = edge_rows(True, near_end)
    x_near, x_far = swap(SFC, x_near_out, x_far_out)

    plan = pl.pallas_call(
        functools.partial(plan_kernel, per_brick, parts),
        in_specs=[pl.BlockSpec(memory_space=pl.ANY)] + [vmem] * 5,
        out_specs=vmem,
        out_shape=shape((16, faces), f32),
        compiler_params=SMALL,
        name="face_plan",
    )(x_near_out, face, cut_cell, face_pressure, owner, tri_local)

    relaxed, message = pl.pallas_call(
        functools.partial(third_kernel, parts),
        in_specs=[vmem] * 15,
        out_specs=[hbm, vmem],
        out_shape=[block, shape((n_y * n_c * n_x, 8 * n_z), f32)],
        scratch_shapes=scratch(padded, edge, edge, block) + [dma((2,))],
        compiler_params=ROOM,
        name="second_step",
    )(jac_rows, plan, partial, walls, source, velocity, dissip, y_near_out, y_far_out, from_near, from_far,
      x_near_out, x_far_out, x_near, x_far)

    got = lax.all_to_all(message, ("y", "core", "blk"), split_axis=0, concat_axis=0, tiled=True)
    turned = pl.pallas_call(
        turn_kernel,
        in_specs=[vmem],
        out_specs=vmem,
        out_shape=shape((8 * n_z, 128), f32),
        compiler_params=SMALL,
        name="turn_words",
    )(got)
    got = lax.all_to_all(turned, "z", split_axis=0, concat_axis=0, tiled=True)
    sensitivity = pl.pallas_call(
        functools.partial(last_kernel, n_y * n_c * n_x),
        in_specs=[vmem],
        out_specs=vmem,
        out_shape=shape((3, TRI_DEV), f32),
        compiler_params=SMALL,
        name="sum_terms",
    )(got)
    return relaxed, sensitivity


def solution(mesh):
    n_sfc, n_blk = mesh.shape["sfc"], mesh.shape["blk"]
    n_z = min(16, n_sfc // 2)
    split = jax.sharding.Mesh(mesh.devices.reshape(n_sfc // (2 * n_z), n_z, 2, n_blk), SFC + ("blk",))
    grid = P(None, SFC, "blk", None)
    both = SFC + ("blk",)
    return jax.shard_map(
        on_device,
        mesh=split,
        in_specs=(grid, grid, grid, P(SFC, "blk", None), P(), P(both), P(both), P(None, both), P(both), P(both),
                  P(both, None), P(both)),
        out_specs=(grid, P(None, both)),
        check_vma=False,
    )
```
